128 devices in a mesh: mem: 4 (over y), lat: 8 (over z_lo, x), lon: 4 (over z_hi, core).
Axes of the slice: x: 4, y: 4, z: 4 (z_hi: 2, z_lo: 2; z = z_hi * 2 + z_lo), core: 2. Of those that a mesh axis runs over, the one named last changes fastest.
Arguments:
- control: float32 [20, 128, 512], P('mem', 'lat', 'lon'), may hold values from -7 to 7
- anomalies: bfloat16 [20, 2, 4, 70, 128, 512], P('mem', None, None, None, 'lat', 'lon'), may hold values from -6 to 6
- diffusivity: float32 [128, 512], P('lat', 'lon'), may hold values from 0.03 to 0.24
- loc_norm: float32 [128, 512], P('lat', 'lon'), may hold values from 0.5 to 1.5
- innovation: float32 [4, 70, 128, 512], P(None, None, 'lat', 'lon'), may hold values from -6 to 6
- obs_precision: float32 [4, 70, 128, 512], P(None, None, 'lat', 'lon'), may hold values from 0.03 to 0.9
- obs_time: int32 [128, 512], P('lat', 'lon'), may hold values from 0 to 1
Outputs:
- gradient: float32 [20, 128, 512], P('mem', 'lat', 'lon')
- cost: float32 [], replicated
The draws below stay inside these ranges and needn't reach their ends.
All inputs are finite; a program needn't handle non-finite values.
Results may differ from the reference program's by a relative error of at most 0.0025.
Values may be sent and summed in bfloat16 or wider, within the bound.
No kernel may reach another device: no remote copies, remote signals or barrier semaphores. Data moves between devices by JAX's collectives and lax.ppermute only.
A program may use at most 64 MiB of HBM per device.

```python
import math
import jax
import jax.numpy as jnp
from jax import lax

FIELDS = 4
LEVELS = 70
TIMES = 2
PASSES = 10
MEMBERS = 20
NLAT = 128
NLON = 512


def draw_control(key, part):
    key = jax.random.fold_in(key, 11)
    member = jnp.arange(MEMBERS, dtype=jnp.float32)[:, None, None]
    spread = jnp.sqrt(1.0 + 2.0 * member / (MEMBERS - 1))
    base = jnp.clip(jax.random.normal(key, (MEMBERS, NLAT, NLON), jnp.float32), -4.0, 4.0)
    return (base * spread).astype(jnp.float32)


def draw_obs_precision(key, part):
    key = jax.random.fold_in(key, 23)
    rows = jnp.arange(NLAT, dtype=jnp.float32)[:, None] / max(NLAT - 1, 1)
    cols = jnp.arange(NLON, dtype=jnp.float32)[None, :] / max(NLON - 1, 1)
    ramp = jnp.exp(jnp.log(3.0) * (rows + cols))
    shape = (FIELDS, LEVELS, NLAT, NLON)
    base = jnp.exp(jax.random.uniform(key, shape, jnp.float32, jnp.log(0.03), jnp.log(0.1)))
    return jnp.clip(base * ramp, 0.03, 0.9).astype(jnp.float32)


def touch_ends(drawn, stream_key, smallest, high):
    index_at = [jax.random.randint(jax.random.fold_in(stream_key, axis), (), 0, length) for axis, length in enumerate(drawn.shape)]
    longest = drawn.shape.index(max(drawn.shape))
    neighbour = index_at[:longest] + [(index_at[longest] + 1) % drawn.shape[longest]] + index_at[longest + 1:]
    return drawn.at[tuple(index_at)].set(smallest).at[tuple(neighbour)].set(high)


def block_levels(rng, extent, shards, least, top_value):
    loudness = 1.0
    for axis_at, parts in shards:
        draws = jax.random.uniform(jax.random.fold_in(jax.random.fold_in(rng, 6), axis_at), (parts,), jnp.float32, least / len(shards), top_value / len(shards))
        loudness = loudness * jnp.repeat(jnp.exp(draws), extent[axis_at] // parts).reshape((-1,) + (1,) * (len(extent) - 1 - axis_at))
    return loudness


def scatter_about(own_key, shape, deviation, most, shards=(), kind=jnp.bfloat16):
    values = jax.random.normal(own_key, shape, jnp.float32) * deviation
    if len(shards) > 0:
        values = block_levels(own_key, shape, shards, -0.22, 0.18) * values
    return jnp.clip(values, min=-most, max=most).astype(kind)


def setup_inputs(seed: int = 0) -> dict:
    streams_of = jax.random.split(jax.random.key(seed), 8)
    return {
        "control": draw_control(jax.random.fold_in(streams_of[7], 71), 0),
        "anomalies": scatter_about(streams_of[1], (MEMBERS, TIMES, FIELDS, LEVELS, NLAT, NLON), 1.0, 6.0, ((0, 4), (4, 8), (5, 4))),
        "diffusivity": jnp.clip(jnp.exp(math.log(0.24) - 2.0794415 * jax.random.uniform(streams_of[2], (NLAT, NLON), jnp.float32) ** block_levels(streams_of[2], (NLAT, NLON), ((0, 8), (1, 4)), -0.2, 0.2)), 0.03, 0.24),
        "loc_norm": jnp.clip(1.0 + 0.1 * jax.random.normal(streams_of[3], (NLAT, NLON), jnp.float32), 0.5, 1.5),
        "innovation": scatter_about(streams_of[4], (FIELDS, LEVELS, NLAT, NLON), 1.0, 6.0, ((2, 8), (3, 4)), jnp.float32),
        "obs_precision": draw_obs_precision(jax.random.fold_in(streams_of[7], 71), 0),
        "obs_time": touch_ends(jax.random.randint(streams_of[6], (NLAT, NLON), 0, TIMES), jax.random.fold_in(streams_of[6], 1), 0, TIMES - 1).astype(jnp.int32),
    }


def laplace(field):
    padded = jnp.pad(field, ((0, 0), (1, 1), (0, 0)))
    upper = padded[:, 2:, :]
    lower = padded[:, :-2, :]
    eastern = jnp.roll(field, -1, axis=2)
    western = jnp.roll(field, 1, axis=2)
    return upper + lower + eastern + western - 4.0 * field

def reference(control, anomalies, diffusivity, loc_norm, innovation, obs_precision, obs_time):
    factor = 1.0 / math.sqrt(MEMBERS - 1)
    spread = control
    for step in range(PASSES):
        spread = spread + diffusivity * laplace(spread)
    weights = (loc_norm * spread).astype(jnp.bfloat16)
    chosen = [(obs_time == t).astype(jnp.float32) for t in range(TIMES)]

    def add_member(total, pair):
        block, weight = pair
        wide = weight.astype(jnp.float32)
        for t in range(TIMES):
            total = total + block[t].astype(jnp.float32) * (wide * chosen[t])
        return (total, None)
    start = jnp.zeros((FIELDS, LEVELS, NLAT, NLON), jnp.float32)
    total, unused = lax.scan(add_member, start, (anomalies, weights))
    increment = factor * total
    misfit = increment - innovation
    scaled = obs_precision * misfit
    residual_sum = jnp.sum(misfit * scaled)
    weighted = scaled.astype(jnp.bfloat16).astype(jnp.float32)

    def pull_member(block):
        result = jnp.zeros((NLAT, NLON), jnp.float32)
        for t in range(TIMES):
            result = result + chosen[t] * lax.optimization_barrier(jnp.sum(block[t].astype(jnp.float32) * weighted, axis=(0, 1)))
        return result
    pulled = factor * lax.map(pull_member, anomalies)
    back = loc_norm * pulled
    for step in range(PASSES):
        back = back + laplace(diffusivity * back)
    gradient = control + back
    cost = 0.5 * (jnp.sum(control * control) + residual_sum) / (MEMBERS * NLAT * NLON)
    return (gradient, cost)
```

```python
import functools
import math

import jax
import jax.numpy as jnp
from jax import lax
from jax.experimental import pallas as pl
from jax.experimental.pallas import tpu as pltpu
from jax.sharding import PartitionSpec as P

F32 = jnp.float32
BF16 = jnp.bfloat16
PASSES = 10
REACH = 10
ROWS, COLS = 16, 128
MEMBERS = 5
PLANES = 280
PIECE = PLANES // 8
CHUNKS = ((0, PIECE),)
MIB = 1 << 20

VMEM_SPEC = pl.BlockSpec(memory_space=pltpu.VMEM)
SMEM_SPEC = pl.BlockSpec(memory_space=pltpu.SMEM)
ANY_SPEC = pl.BlockSpec(memory_space=pl.ANY)


def call(body, outs, args, specs, scratch=(), limit=8 * MIB, us=1.0, aliases=None):
    return pl.pallas_call(
        body,
        out_shape=outs,
        in_specs=specs,
        out_specs=[VMEM_SPEC] * len(outs),
        scratch_shapes=list(scratch),
        input_output_aliases=aliases or {},
        compiler_params=pltpu.CompilerParams(vmem_limit_bytes=limit),
        cost_estimate=pl.CostEstimate(
            flops=int(us * 1e6), bytes_accessed=int(us * 3e6), transcendentals=0
        ),
    )(*args)


def swap(cells, axis, odd):
    count = lax.axis_size(axis)
    pairs = []
    for i in range(count):
        to = i ^ 1 if not odd else ((i + 1) ^ 1) - 1
        pairs.append((i, to % count))
    return lax.ppermute(cells, axis, pairs)


def trade(cells, axis, bit):
    count = lax.axis_size(axis)
    return lax.ppermute(cells, axis, [(i, i ^ bit) for i in range(count)])


def pack_body(fields, mask_edges, ids, own, even, odd, ext, packed):
    lat = ids[1]
    is_even = lax.rem(lat, 2) == 0
    lane = lax.broadcasted_iota(jnp.int32, (3 * ROWS, COLS), 1)
    out = jnp.zeros((3 * ROWS, COLS), F32)
    for f in range(fields):
        a, b = even[f], odd[f]
        up = jnp.where(is_even, b, a)
        down = jnp.where(is_even, a, b)
        if mask_edges:
            up = jnp.where(lat == 0, 0.0, up)
            down = jnp.where(lat == lax.axis_size("lat") - 1, 0.0, down)
        whole = jnp.concatenate([up, own[f], down], axis=0)
        ext[f] = whole
        at = 2 * REACH * f
        turned = pltpu.roll(whole, (at + REACH) % COLS, 1)
        out = jnp.where((lane >= at) & (lane < at + 2 * REACH), turned, out)
    packed[...] = out


def pack(fields, mask_edges, ids, own, even, odd):
    return call(
        functools.partial(pack_body, fields, mask_edges),
        [pltpu.VMEM((fields, 3 * ROWS, COLS), F32), pltpu.VMEM((3 * ROWS, COLS), F32)],
        (ids, own, even, odd),
        [SMEM_SPEC] + [VMEM_SPEC] * 3,
        us=0.3,
    )


def halo_of(fields, ids, even, odd):
    is_even = lax.rem(ids[2], 2) == 0
    lane = lax.broadcasted_iota(jnp.int32, (3 * ROWS, COLS), 1)
    west = lane < 0
    for f in range(fields):
        at = 2 * REACH * f
        west = west | ((lane >= at) & (lane < at + REACH))
    a, b = even[...], odd[...]
    return jnp.where(west, jnp.where(is_even, b, a), jnp.where(is_even, a, b))


def spread_halo(halo, f):
    return pltpu.roll(halo, (2 * COLS - REACH - 2 * REACH * f) % COLS, 1)


def lap(own, side):
    rows = own.shape[0]
    lane = lax.broadcasted_iota(jnp.int32, own.shape, 1)
    first, last = lane == 0, lane == COLS - 1
    own_w, side_w = pltpu.roll(own, 1, 1), pltpu.roll(side, 1, 1)
    own_e, side_e = pltpu.roll(own, COLS - 1, 1), pltpu.roll(side, COLS - 1, 1)

    def total(v, west, east):
        above = pltpu.roll(v, 1, 0)
        below = pltpu.roll(v, rows - 1, 0)
        return (above + below) + (west + east) - 4.0 * v

    return (
        total(own, jnp.where(first, side_w, own_w), jnp.where(last, side_e, own_e)),
        total(side, jnp.where(first, own_w, side_w), jnp.where(last, own_e, side_e)),
    )


def forward_pass(state, rate):
    a, b = lap(*state)
    return state[0] + rate[0] * a, state[1] + rate[1] * b


def adjoint_pass(state, rate):
    a, b = lap(state[0] * rate[0], state[1] * rate[1])
    return state[0] + a, state[1] + b


def sweep(step, state, rate):
    cut = ROWS // 2
    for _ in range(2):
        state = step(state, rate)
    state = tuple(v[cut:-cut] for v in state)
    rate = tuple(v[cut:-cut] for v in rate)
    state = lax.fori_loop(0, PASSES - 2, lambda _, s: step(s, rate), state)
    return state[0][ROWS - cut : -(ROWS - cut)]


def select_body(anomalies, obs_time, innovation, precision, ids, sel, inn_own, prec_own, buf, sems, own_sems):
    parts = buf.shape[2] // 56
    for m in range(MEMBERS):
        for p in range(parts):
            at = pl.ds(56 * p, 56)
            pltpu.make_async_copy(anomalies.at[m, :, at], buf.at[m, :, at], sems.at[m * parts + p]).start()
    mem = ids[0]
    own_copies = []
    for n, start in enumerate(own_starts(mem)):
        for k, (src, dst) in enumerate(((innovation, inn_own), (precision, prec_own))):
            copy = pltpu.make_async_copy(
                src.at[pl.ds(start, PIECE)], dst.at[pl.ds(n * PIECE, PIECE)], own_sems.at[2 * n + k]
            )
            copy.start()
            own_copies.append(copy)
    at_zero = obs_time[...].astype(F32).astype(BF16) == 0
    for m in range(MEMBERS):

        def part(p, carry):
            at = pl.ds(56 * p, 56)
            pltpu.make_async_copy(anomalies.at[m, :, at], buf.at[m, :, at], sems.at[m * parts + p]).wait()

            def plane(r, c):
                r = 56 * p + r
                sel[m, r] = jnp.where(at_zero, buf[m, 0, r], buf[m, 1, r])
                return c

            return lax.fori_loop(0, 56, plane, carry, unroll=8)

        lax.fori_loop(0, parts, part, 0)
    for copy in own_copies:
        copy.wait()


def keeps(mem):
    high = lax.div(mem, 2)
    low = lax.rem(mem, 2)
    return (lax.rem(high + low, 2), high), (high, low)


def start_of(group, half, quarter):
    return 4 * PIECE * group + 2 * PIECE * half + PIECE * quarter


def own_starts(mem):
    return [start_of(g, *k) for g, k in enumerate(keeps(mem))]


def add_members(sel, w, start, count, store):
    ws = [w[m] for m in range(MEMBERS)]

    def plane(r, c):
        total = sel[0, start + r].astype(F32) * ws[0]
        for m in range(1, MEMBERS):
            total = total + sel[m, start + r].astype(F32) * ws[m]
        store(r, total)
        return c

    lax.fori_loop(0, count, plane, 0, unroll=5 if count % 5 == 0 else 1)


def first_sends(chunk, ids, sel, w, send1, send2):
    first, count = chunk
    for g, (out, (half, _)) in enumerate(zip((send1, send2), keeps(ids[0]))):
        for q in range(2):

            def store(r, total, out=out, q=q):
                out[q * count + r] = total.astype(BF16)

            add_members(sel, w, start_of(g, 1 - half, q) + first, count, store)


def forward_body(chunk, ids, ext, even, odd, loc_norm, sel, w, rate, terms, send1, send2):
    halo = halo_of(MEMBERS + 1, ids, even, odd)
    lane = lax.broadcasted_iota(jnp.int32, (3 * ROWS, COLS), 1)
    near = (lane < REACH) | (lane >= COLS - REACH)
    rate_own = ext[MEMBERS]
    rate_side = jnp.where(near, spread_halo(halo, MEMBERS), 0.0)
    rate[0] = rate_own
    rate[1] = rate_side
    squares = jnp.zeros((ROWS, COLS), F32)
    for m in range(MEMBERS):
        own = ext[m]
        mine = own[ROWS : 2 * ROWS]
        squares = squares + mine * mine
        spread = sweep(forward_pass, (own, spread_halo(halo, m)), (rate_own, rate_side))
        w[m] = (loc_norm[...] * spread).astype(BF16).astype(F32)
    terms[...] = squares[:8] + squares[8:]
    first_sends(chunk, ids, sel, w, send1, send2)


def own_body(chunk, ids, sel, w, own1, own2):
    first, count = chunk
    for g, (out, (half, _)) in enumerate(zip((own1, own2), keeps(ids[0]))):
        for q in range(2):

            def store(r, total, out=out, q=q):
                out[q * count + r] = total

            add_members(sel, w, start_of(g, half, q) + first, count, store)


def second_body(count, ids, own1, own2, got1, got2, send1, send2):
    for own, got, out, (_, quarter) in zip((own1, own2), (got1, got2), (send1, send2), keeps(ids[0])):
        at = (1 - quarter) * count

        def plane(r, c, own=own, got=got, out=out, at=at):
            out[r] = (own[at + r] + got[at + r].astype(F32)).astype(BF16)
            return c

        lax.fori_loop(0, count, plane, 0, unroll=5 if count % 5 == 0 else 1)


def misfit_body(chunk, factor, ids, own1, own2, got1, got2, last1, last2, inn, prec, terms, weighted, new_terms):
    first, count = chunk
    total = jnp.zeros((ROWS, COLS), F32)
    for g, (own, got, last, (_, quarter)) in enumerate(
        zip((own1, own2), (got1, got2), (last1, last2), keeps(ids[0]))
    ):
        at = quarter * count

        def plane(r, c, own=own, got=got, last=last, at=at, g=g):
            sums = own[at + r] + got[at + r].astype(F32) + last[r].astype(F32)
            misfit = factor * sums - inn[g * PIECE + first + r]
            scaled = prec[g * PIECE + first + r] * misfit
            weighted[g * count + r] = scaled.astype(BF16)
            return c + misfit * scaled

        total = lax.fori_loop(0, count, plane, total, unroll=5 if count % 5 == 0 else 1)
    new_terms[...] = terms[...] + (total[:8] + total[8:])


def pull(sel, parts, acc):
    for ref, at, start, count in parts:

        def plane(r, acc, ref=ref, at=at, start=start):
            x = ref[at + r].astype(F32)
            return tuple(acc[m] + sel[m, start + r].astype(F32) * x for m in range(MEMBERS))

        acc = lax.fori_loop(0, count, plane, acc, unroll=5 if count % 5 == 0 else 1)
    return acc


def pieces_of(stage, chunk, mem, refs):
    first, count = chunk
    (h1, q1), (h2, q2) = keeps(mem)
    if stage == "own":
        where = [(0, h1, q1), (1, h2, q2)]
        blocks = [(refs[0], 0), (refs[0], count)]
    elif stage == "near":
        where = [(0, 1 - h1, q1), (1, h2, 1 - q2), (0, h1, 1 - q1), (1, 1 - h2, 1 - q2)]
        blocks = [(refs[0], 0), (refs[0], count), (refs[1], 0), (refs[1], count)]
    else:
        where = [(0, 1 - h1, 1 - q1), (1, 1 - h2, q2)]
        blocks = [(refs[0], 0), (refs[1], 0)]
    return [(ref, at, start_of(*place) + first, count) for (ref, at), place in zip(blocks, where)]


def pull_body(stage, chunk, ids, sel, old, *rest):
    refs, new = rest[:-1], rest[-1]
    acc = tuple(old[m] for m in range(MEMBERS))
    acc = pull(sel, pieces_of(stage, chunk, ids[0], refs), acc)
    for m in range(MEMBERS):
        new[m] = acc[m]


def first_pull_body(chunk, ids, sel, ref, new):
    acc = tuple(jnp.zeros((ROWS, COLS), F32) for _ in range(MEMBERS))
    acc = pull(sel, pieces_of("own", chunk, ids[0], [ref]), acc)
    for m in range(MEMBERS):
        new[m] = acc[m]


def last_pull_body(chunk, factor, ids, sel, old, loc_norm, ref1, ref2, new):
    acc = tuple(old[m] for m in range(MEMBERS))
    acc = pull(sel, pieces_of("far", chunk, ids[0], [ref1, ref2]), acc)
    for m in range(MEMBERS):
        new[m] = loc_norm[...] * (factor * acc[m])


def adjoint_body(ids, ext, even, odd, rate, control, out):
    halo = halo_of(MEMBERS, ids, even, odd)
    rates = (rate[0], rate[1])
    for m in range(MEMBERS):
        out[m] = control[m] + sweep(adjoint_pass, (ext[m], spread_halo(halo, m)), rates)


def on_device(control, anomalies, diffusivity, loc_norm, innovation, obs_precision, obs_time):
    members = MEMBERS * lax.axis_size("mem")
    cells = members * ROWS * COLS * lax.axis_size("lat") * lax.axis_size("lon")
    factor = 1.0 / math.sqrt(members - 1)
    ids = jnp.stack([lax.axis_index(a) for a in ("mem", "lat", "lon")]).astype(jnp.int32)
    anomalies = anomalies.reshape(MEMBERS, 2, PLANES, ROWS, COLS)
    innovation = innovation.reshape(PLANES, ROWS, COLS)
    obs_precision = obs_precision.reshape(PLANES, ROWS, COLS)
    block = (MEMBERS, ROWS, COLS)

    fields = jnp.concatenate([control, diffusivity[None]], axis=0)
    even, odd = swap(fields, "lat", False), swap(fields, "lat", True)
    sel, inn, prec = call(
        select_body,
        [
            pltpu.VMEM((MEMBERS, PLANES, ROWS, COLS), BF16),
            pltpu.VMEM((2 * PIECE, ROWS, COLS), F32),
            pltpu.VMEM((2 * PIECE, ROWS, COLS), F32),
        ],
        (anomalies, obs_time, innovation, obs_precision, ids),
        [ANY_SPEC, VMEM_SPEC, ANY_SPEC, ANY_SPEC, SMEM_SPEC],
        scratch=[
            pltpu.VMEM((MEMBERS, 2, PLANES, ROWS, COLS), BF16),
            pltpu.SemaphoreType.DMA((25,)),
            pltpu.SemaphoreType.DMA((4,)),
        ],
        limit=24 * MIB,
        us=4.0,
    )
    ext, packed = pack(MEMBERS + 1, True, ids, fields, even, odd)
    even, odd = swap(packed, "lon", False), swap(packed, "lon", True)

    def sends(count):
        return [pltpu.VMEM((2 * count, ROWS, COLS), BF16)] * 2

    w = None
    got, own = [], []
    for chunk in CHUNKS:
        if w is None:
            w, rate, terms, *send = call(
                functools.partial(forward_body, chunk),
                [
                    pltpu.VMEM(block, F32),
                    pltpu.VMEM((2, 3 * ROWS, COLS), F32),
                    pltpu.VMEM((8, COLS), F32),
                    *sends(chunk[1]),
                ],
                (ids, ext, even, odd, loc_norm, sel),
                [SMEM_SPEC] + [VMEM_SPEC] * 5,
                us=2.0,
            )
        else:
            send = call(
                functools.partial(first_sends, chunk),
                sends(chunk[1]),
                (ids, sel, w),
                [SMEM_SPEC] + [VMEM_SPEC] * 2,
                us=0.5,
            )
        got.append((swap(send[0], "mem", False), swap(send[1], "mem", True)))
        own.append(
            call(
                functools.partial(own_body, chunk),
                [pltpu.VMEM((2 * chunk[1], ROWS, COLS), F32)] * 2,
                (ids, sel, w),
                [SMEM_SPEC] + [VMEM_SPEC] * 2,
                us=0.5,
            )
        )
    last = []
    for i, (_, count) in enumerate(CHUNKS):
        send = call(
            functools.partial(second_body, count),
            [pltpu.VMEM((count, ROWS, COLS), BF16)] * 2,
            (ids, *own[i], *got[i]),
            [SMEM_SPEC] + [VMEM_SPEC] * 4,
            us=0.2,
        )
        last.append((swap(send[0], "mem", True), swap(send[1], "mem", False)))
    weighted, near = [], []
    for i, chunk in enumerate(CHUNKS):
        piece, terms = call(
            functools.partial(misfit_body, chunk, factor),
            [pltpu.VMEM((2 * chunk[1], ROWS, COLS), BF16), pltpu.VMEM((8, COLS), F32)],
            (ids, *own[i], *got[i], *last[i], inn, prec, terms),
            [SMEM_SPEC] + [VMEM_SPEC] * 9,
            us=0.3,
        )
        weighted.append(piece)
        near.append((swap(piece, "mem", False), swap(piece, "mem", True)))
    for axis, bit in (("lon", 1), ("lat", 1), ("mem", 1), ("lat", 4), ("lat", 2), ("lon", 2), ("mem", 2)):
        terms = terms + trade(terms, axis, bit)
    cost = jnp.sum(terms) * (0.5 / cells)

    acc = None
    for i, chunk in enumerate(CHUNKS):
        if acc is None:
            body, extra, specs = functools.partial(first_pull_body, chunk), (), 2
        else:
            body, extra, specs = functools.partial(pull_body, "own", chunk), (acc,), 3
        (acc,) = call(
            body,
            [pltpu.VMEM(block, F32)],
            (ids, sel, *extra, weighted[i]),
            [SMEM_SPEC] + [VMEM_SPEC] * specs,
            us=0.3,
        )
    far = []
    for i, chunk in enumerate(CHUNKS):
        a, b = near[i]
        far.append((swap(b[: chunk[1]], "mem", False), swap(a[chunk[1] :], "mem", True)))
        (acc,) = call(
            functools.partial(pull_body, "near", chunk),
            [pltpu.VMEM(block, F32)],
            (ids, sel, acc, a, b),
            [SMEM_SPEC] + [VMEM_SPEC] * 4,
            us=0.6,
        )
    for i, chunk in enumerate(CHUNKS):
        if i < len(CHUNKS) - 1:
            (acc,) = call(
                functools.partial(pull_body, "far", chunk),
                [pltpu.VMEM(block, F32)],
                (ids, sel, acc, *far[i]),
                [SMEM_SPEC] + [VMEM_SPEC] * 4,
                us=0.3,
            )
        else:
            (source,) = call(
                functools.partial(last_pull_body, chunk, factor),
                [pltpu.VMEM(block, F32)],
                (ids, sel, acc, loc_norm, *far[i]),
                [SMEM_SPEC] + [VMEM_SPEC] * 5,
                us=0.3,
            )
    even, odd = swap(source, "lat", False), swap(source, "lat", True)
    ext, packed = pack(MEMBERS, False, ids, source, even, odd)
    even, odd = swap(packed, "lon", False), swap(packed, "lon", True)
    (gradient,) = call(
        adjoint_body,
        [jax.ShapeDtypeStruct(block, F32)],
        (ids, ext, even, odd, rate, control),
        [SMEM_SPEC] + [VMEM_SPEC] * 5,
        us=1.5,
    )
    return gradient, cost


def solution(mesh):
    return jax.shard_map(
        on_device,
        mesh=mesh,
        in_specs=(
            P("mem", "lat", "lon"),
            P("mem", None, None, None, "lat", "lon"),
            P("lat", "lon"),
            P("lat", "lon"),
            P(None, None, "lat", "lon"),
            P(None, None, "lat", "lon"),
            P("lat", "lon"),
        ),
        out_specs=(P("mem", "lat", "lon"), P()),
        check_vma=False,
    )
```

```python
import functools
import math

import jax
import jax.numpy as jnp
from jax import lax
from jax.experimental import pallas as pl
from jax.experimental.pallas import tpu as pltpu
from jax.sharding import PartitionSpec as P

F32 = jnp.float32
BF16 = jnp.bfloat16
PASSES = 10
REACH = 10
ROWS, COLS = 16, 128
MEMBERS = 5
PLANES = 280
PIECE = PLANES // 8
CHUNKS = ((0, 20), (20, 15))
MIB = 1 << 20

VMEM_SPEC = pl.BlockSpec(memory_space=pltpu.VMEM)
ANY_SPEC = pl.BlockSpec(memory_space=pl.ANY)


def call(body, outs, args, specs, scratch=(), limit=8 * MIB, us=1.0, aliases=None):
    def placed(*refs):
        body([lax.axis_index(a) for a in ("mem", "lat", "lon")], *refs)

    return pl.pallas_call(
        placed,
        out_shape=outs,
        in_specs=specs,
        out_specs=[VMEM_SPEC] * len(outs),
        scratch_shapes=list(scratch),
        input_output_aliases=aliases or {},
        compiler_params=pltpu.CompilerParams(vmem_limit_bytes=limit),
        cost_estimate=pl.CostEstimate(
            flops=int(us * 1e6), bytes_accessed=int(us * 3e6), transcendentals=0
        ),
    )(*args)


def in_hbm(cells):
    return pltpu.with_memory_space_constraint(cells, pltpu.HBM)


def swap(cells, axis, odd):
    count = lax.axis_size(axis)
    pairs = []
    for i in range(count):
        to = i ^ 1 if not odd else ((i + 1) ^ 1) - 1
        pairs.append((i, to % count))
    return lax.ppermute(cells, axis, pairs)


def trade(cells, axes, to):
    return lax.ppermute(cells, axes, list(enumerate(to)))


def pack_body(fields, mask_edges, ids, own, even, odd, *rest):
    if len(rest) > 2:
        terms, got, both, ext, packed, new_terms = rest
        new_terms[...] = (terms[...] + even[fields, :8]) + (got[...] + both[...])
    else:
        ext, packed = rest
    lat = ids[1]
    is_even = lax.rem(lat, 2) == 0
    lane = lax.broadcasted_iota(jnp.int32, (3 * ROWS, COLS), 1)
    out = jnp.zeros((3 * ROWS, COLS), F32)
    for f in range(fields):
        a, b = even[f], odd[f]
        up = jnp.where(is_even, b, a)
        down = jnp.where(is_even, a, b)
        if mask_edges:
            up = jnp.where(lat == 0, 0.0, up)
            down = jnp.where(lat == 7, 0.0, down)
        whole = jnp.concatenate([up, own[f], down], axis=0)
        ext[f] = whole
        at = 2 * REACH * f
        turned = pltpu.roll(whole, (at + REACH) % COLS, 1)
        out = jnp.where((lane >= at) & (lane < at + 2 * REACH), turned, out)
    packed[...] = out


def pack(fields, mask_edges, own, even, odd, terms=()):
    return call(
        functools.partial(pack_body, fields, mask_edges),
        [pltpu.VMEM((fields, 3 * ROWS, COLS), F32), pltpu.VMEM((3 * ROWS, COLS), F32)]
        + [pltpu.VMEM((8, COLS), F32)] * (1 if terms else 0),
        (own, even, odd, *terms),
        [VMEM_SPEC] * (3 + len(terms)),
        us=0.3,
    )


def group(lane, m):
    return (lane >= 2 * REACH * m) & (lane < 2 * REACH * (m + 1))


def halo_of(fields, ids, even, odd):
    is_even = lax.rem(ids[2], 2) == 0
    lane = lax.broadcasted_iota(jnp.int32, (3 * ROWS, COLS), 1)
    west = lane < 0
    for f in range(fields):
        at = 2 * REACH * f
        west = west | ((lane >= at) & (lane < at + REACH))
    a, b = even[...], odd[...]
    return jnp.where(west, jnp.where(is_even, b, a), jnp.where(is_even, a, b))


def lap(own, side):
    rows = side.shape[0]
    lane = lax.broadcasted_iota(jnp.int32, side.shape, 1)
    inner_w, inner_e = lane < 0, lane < 0
    for m in range(MEMBERS):
        at = 2 * REACH * m + REACH
        inner_w, inner_e = inner_w | (lane == at - 1), inner_e | (lane == at)

    def total(v, west, east):
        above = pltpu.roll(v, 1, 0)
        below = pltpu.roll(v, rows - 1, 0)
        return (above + below) + (west + east) - 4.0 * v

    west_side, east_side = side, side
    out = []
    for m in range(MEMBERS):
        at = 2 * REACH * m + REACH
        v = own[m]
        ends = pltpu.roll(side, COLS - at, 1)
        west = pltpu.roll(jnp.where(lane == COLS - 1, ends, v), 1, 1)
        east = pltpu.roll(jnp.where(lane == 0, ends, v), COLS - 1, 1)
        out.append(total(v, west, east))
        edges = pltpu.roll(v, at, 1)
        west_side = jnp.where(lane == at - 1, edges, west_side)
        east_side = jnp.where(lane == at, edges, east_side)
    return out, total(side, pltpu.roll(west_side, 1, 1), pltpu.roll(east_side, COLS - 1, 1))


def forward_pass(state, rate):
    (own, side), (rate_own, rate_side) = state, rate
    a, b = lap(own, side)
    return [v + rate_own * x for v, x in zip(own, a)], side + rate_side * b


def adjoint_pass(state, rate):
    (own, side), (rate_own, rate_side) = state, rate
    a, b = lap([rate_own * v for v in own], rate_side * side)
    return [v + x for v, x in zip(own, a)], side + b


def sweep(step, own, side, rate):
    cut = ROWS // 2
    state = (own, side)
    for _ in range(2):
        state = step(state, rate)
    own, side = [v[cut:-cut] for v in state[0]], state[1][cut:-cut]
    rate = tuple(v[cut:-cut] for v in rate)
    own, side = lax.fori_loop(0, PASSES - 2, lambda _, s: step(s, rate), (own, side))
    return [v[ROWS - cut : -(ROWS - cut)] for v in own]


SPLIT = (0, 3, MEMBERS)
STEP = 56


def select_body(first, ids, anomalies, obs_time, *rest):
    if first == 0:
        sel, buf, when, sems, own_sems = rest
        own = ()
    else:
        innovation, precision, sel, inn_own, prec_own, buf, when, sems, own_sems = rest
        own = ((innovation, inn_own), (precision, prec_own))
    time_copy = pltpu.make_async_copy(obs_time, when, own_sems.at[4])
    time_copy.start()
    parts = PLANES // STEP
    members = sel.shape[0]
    for m in range(members):
        for p in range(parts):
            at = pl.ds(STEP * p, STEP)
            pltpu.make_async_copy(anomalies.at[first + m, :, at], buf.at[m, :, at], sems.at[m * parts + p]).start()
    own_copies = []
    for k, (src, dst) in enumerate(own):
        for n, start in enumerate(own_starts(ids[0])):
            copy = pltpu.make_async_copy(
                src.at[pl.ds(start, PIECE)], dst.at[pl.ds(n * PIECE, PIECE)], own_sems.at[2 * n + k]
            )
            copy.start()
            own_copies.append(copy)
    time_copy.wait()
    at_zero = when[...].astype(F32).astype(BF16) == 0
    for m in range(members):

        def part(p, carry):
            at = pl.ds(STEP * p, STEP)
            pltpu.make_async_copy(anomalies.at[first + m, :, at], buf.at[m, :, at], sems.at[m * parts + p]).wait()

            def plane(r, c):
                r = STEP * p + r
                sel[m, r] = jnp.where(at_zero, buf[m, 0, r], buf[m, 1, r])
                return c

            return lax.fori_loop(0, STEP, plane, carry, unroll=8)

        lax.fori_loop(0, parts, part, 0)
    for copy in own_copies:
        copy.wait()


def select(part, anomalies, obs_time, own=()):
    first, end = SPLIT[part], SPLIT[part + 1]
    members = end - first
    return call(
        functools.partial(select_body, first),
        [pltpu.VMEM((members, PLANES, ROWS, COLS), BF16)]
        + [pltpu.VMEM((2 * PIECE, ROWS, COLS), F32)] * (2 if own else 0),
        (anomalies, obs_time, *own),
        [ANY_SPEC, ANY_SPEC] + ([ANY_SPEC, ANY_SPEC] if own else []),
        scratch=[
            pltpu.VMEM((members, 2, PLANES, ROWS, COLS), BF16),
            pltpu.VMEM((ROWS, COLS), jnp.int32),
            pltpu.SemaphoreType.DMA((members * (PLANES // STEP),)),
            pltpu.SemaphoreType.DMA((5,)),
        ],
        limit=16 * MIB,
        us=2.5,
    )


def keeps(mem):
    high = lax.div(mem, 2)
    low = lax.rem(mem, 2)
    return (lax.rem(high + low, 2), high), (high, low)


def start_of(group, half, quarter):
    return 4 * PIECE * group + 2 * PIECE * half + PIECE * quarter


def own_starts(mem):
    return [start_of(g, *k) for g, k in enumerate(keeps(mem))]


def member(sels, m, plane):
    return (sels[0][m, plane] if m < SPLIT[1] else sels[1][m - SPLIT[1], plane]).astype(F32)


def add_members(sels, w, start, count, store):
    ws = [w[m] for m in range(MEMBERS)]

    def plane(r, c):
        total = member(sels, 0, start + r) * ws[0]
        for m in range(1, MEMBERS):
            total = total + member(sels, m, start + r) * ws[m]
        store(r, total)
        return c

    lax.fori_loop(0, count, plane, 0, unroll=5 if count % 5 == 0 else 1)


def sends(chunk, ids, sels, w, send1, send2):
    first, count = chunk
    for g, (out, (half, _)) in enumerate(zip((send1, send2), keeps(ids[0]))):
        for q in range(2):

            def store(r, total, out=out, q=q):
                out[q * count + r] = total.astype(BF16)

            add_members(sels, w, start_of(g, 1 - half, q) + first, count, store)


def stays(chunk, ids, sels, w, own1, own2):
    first, count = chunk
    for g, (out, (half, _)) in enumerate(zip((own1, own2), keeps(ids[0]))):
        for q in range(2):

            def store(r, total, out=out, q=q):
                out[q * count + r] = total

            add_members(sels, w, start_of(g, half, q) + first, count, store)


def middle_body(chunk, next_chunk, ids, sel0, sel1, w, own1, own2, *rest):
    if rest:
        sends(next_chunk, ids, (sel0, sel1), w, *rest)
    stays(chunk, ids, (sel0, sel1), w, own1, own2)


def forward_body(chunk, ids, ext, even, odd, loc_norm, sel0, sel1, w, rate, terms, send1, send2):
    halo = halo_of(MEMBERS + 1, ids, even, odd)
    lane = lax.broadcasted_iota(jnp.int32, (3 * ROWS, COLS), 1)
    side = jnp.where(lane < 2 * REACH * MEMBERS, halo, 0.0)
    rate_side = jnp.zeros((3 * ROWS, COLS), F32)
    for m in range(MEMBERS):
        turned = pltpu.roll(halo, (COLS - 2 * REACH * (MEMBERS - m)) % COLS, 1)
        rate_side = jnp.where(group(lane, m), turned, rate_side)
    rate[0] = ext[MEMBERS]
    rate[1] = rate_side
    squares = jnp.zeros((ROWS, COLS), F32)
    for m in range(MEMBERS):
        mine = ext[m, ROWS : 2 * ROWS]
        squares = squares + mine * mine
    terms[...] = squares[:8] + squares[8:]
    spread = sweep(forward_pass, [ext[m] for m in range(MEMBERS)], side, (ext[MEMBERS], rate_side))
    for m in range(MEMBERS):
        w[m] = (loc_norm[...] * spread[m]).astype(BF16).astype(F32)
    sends(chunk, ids, (sel0, sel1), w, send1, send2)


def second_body(count, ids, own1, own2, got1, got2, send1, send2):
    for own, got, out, (_, quarter) in zip((own1, own2), (got1, got2), (send1, send2), keeps(ids[0])):
        at = (1 - quarter) * count

        def plane(r, c, own=own, got=got, out=out, at=at):
            out[r] = (own[at + r] + got[at + r].astype(F32)).astype(BF16)
            return c

        lax.fori_loop(0, count, plane, 0, unroll=5 if count % 5 == 0 else 1)


def misfit_body(chunk, factor, ids, own1, own2, got1, got2, last1, last2, inn, prec, terms, weighted, new_terms):
    first, count = chunk
    total = jnp.zeros((ROWS, COLS), F32)
    for g, (own, got, last, (_, quarter)) in enumerate(
        zip((own1, own2), (got1, got2), (last1, last2), keeps(ids[0]))
    ):
        at = quarter * count

        def plane(r, c, own=own, got=got, last=last, at=at, g=g):
            sums = own[at + r] + got[at + r].astype(F32) + last[r].astype(F32)
            misfit = factor * sums - inn[g * PIECE + first + r]
            scaled = prec[g * PIECE + first + r] * misfit
            weighted[g * count + r] = scaled.astype(BF16)
            return c + misfit * scaled

        total = lax.fori_loop(0, count, plane, total, unroll=5 if count % 5 == 0 else 1)
    new_terms[...] = terms[...] + (total[:8] + total[8:])


def pull(sels, parts, acc):
    for ref, at, start, count in parts:

        def plane(r, acc, ref=ref, at=at, start=start):
            x = ref[at + r].astype(F32)
            return tuple(acc[m] + member(sels, m, start + r) * x for m in range(MEMBERS))

        acc = lax.fori_loop(0, count, plane, acc, unroll=5 if count % 5 == 0 else 1)
    return acc


def pieces_of(stage, chunk, mem, refs):
    first, count = chunk
    (h1, q1), (h2, q2) = keeps(mem)
    if stage == "own":
        where = [(0, h1, q1), (1, h2, q2)]
        blocks = [(refs[0], 0), (refs[0], count)]
    elif stage == "near":
        where = [(0, 1 - h1, q1), (1, h2, 1 - q2), (0, h1, 1 - q1), (1, 1 - h2, 1 - q2)]
        blocks = [(refs[0], 0), (refs[0], count), (refs[1], 0), (refs[1], count)]
    else:
        where = [(0, 1 - h1, 1 - q1), (1, 1 - h2, q2)]
        blocks = [(refs[0], 0), (refs[1], 0)]
    return [(ref, at, start_of(*place) + first, count) for (ref, at), place in zip(blocks, where)]


def own_pull_body(ids, sel0, sel1, *rest):
    refs, new = rest[:-1], rest[-1]
    acc = tuple(jnp.zeros((ROWS, COLS), F32) for _ in range(MEMBERS))
    for chunk, ref in zip(CHUNKS, refs):
        acc = pull((sel0, sel1), pieces_of("own", chunk, ids[0], [ref]), acc)
    for m in range(MEMBERS):
        new[m] = acc[m]


def near_pull_body(chunk, ids, sel0, sel1, old, ref1, ref2, new):
    acc = tuple(old[m] for m in range(MEMBERS))
    acc = pull((sel0, sel1), pieces_of("near", chunk, ids[0], [ref1, ref2]), acc)
    for m in range(MEMBERS):
        new[m] = acc[m]


def far_pull_body(factor, ids, sel0, sel1, old, loc_norm, terms, got, *rest):
    refs, new, new_terms = rest[:-2], rest[-2], rest[-1]
    acc = tuple(old[m] for m in range(MEMBERS))
    for i, chunk in enumerate(CHUNKS):
        acc = pull((sel0, sel1), pieces_of("far", chunk, ids[0], refs[2 * i : 2 * i + 2]), acc)
    for m in range(MEMBERS):
        new[m] = loc_norm[...] * (factor * acc[m])
    summed = terms[...] + got[...]
    new_terms[...] = summed
    new[MEMBERS, :8] = summed
    new[MEMBERS, 8:] = jnp.zeros((ROWS - 8, COLS), F32)


def adjoint_body(scale, ids, ext, even, odd, rate, control, terms, got1, got2, got3, out, cost):
    total = (terms[...] + got1[...]) + (got2[...] + got3[...])
    cost[...] = jnp.broadcast_to(jnp.sum(total) * scale, (1, COLS))
    side = halo_of(MEMBERS, ids, even, odd)
    back = sweep(adjoint_pass, [ext[m] for m in range(MEMBERS)], side, (rate[0], rate[1]))
    for m in range(MEMBERS):
        out[m] = control[m] + back[m]


def on_device(control, anomalies, diffusivity, loc_norm, innovation, obs_precision, obs_time):
    members = MEMBERS * lax.axis_size("mem")
    cells = members * ROWS * COLS * lax.axis_size("lat") * lax.axis_size("lon")
    factor = 1.0 / math.sqrt(members - 1)
    obs_time = in_hbm(obs_time)
    anomalies = in_hbm(anomalies.reshape(MEMBERS, 2, PLANES, ROWS, COLS))
    innovation = in_hbm(innovation.reshape(PLANES, ROWS, COLS))
    obs_precision = in_hbm(obs_precision.reshape(PLANES, ROWS, COLS))
    block = (MEMBERS, ROWS, COLS)

    fields = jnp.concatenate([control, diffusivity[None]], axis=0)
    even, odd = swap(fields, "lat", False), swap(fields, "lat", True)
    (sel0,) = select(0, anomalies, obs_time)
    even, odd, sel0 = lax.optimization_barrier((even, odd, sel0))
    ext, packed = pack(MEMBERS + 1, True, fields, even, odd)
    even, odd = swap(packed, "lon", False), swap(packed, "lon", True)
    sel1, inn, prec = select(1, anomalies, obs_time, (innovation, obs_precision))
    even, odd, sel1 = lax.optimization_barrier((even, odd, sel1))

    def sent(count):
        return [pltpu.VMEM((2 * count, ROWS, COLS), BF16)] * 2

    tile = pltpu.VMEM((8, COLS), F32)
    w, rate, terms, *send = call(
        functools.partial(forward_body, CHUNKS[0]),
        [pltpu.VMEM(block, F32), pltpu.VMEM((2, 3 * ROWS, COLS), F32), tile, *sent(CHUNKS[0][1])],
        (ext, even, odd, loc_norm, sel0, sel1),
        [VMEM_SPEC] * 6,
        us=2.0,
    )
    got, own = [], []
    for i, chunk in enumerate(CHUNKS):
        got.append((swap(send[0], "mem", False), swap(send[1], "mem", True)))
        more = CHUNKS[i + 1] if i + 1 < len(CHUNKS) else None
        own1, own2, *send = call(
            functools.partial(middle_body, chunk, more),
            [pltpu.VMEM((2 * chunk[1], ROWS, COLS), F32)] * 2 + (sent(more[1]) if more else []),
            (sel0, sel1, w),
            [VMEM_SPEC] * 3,
            us=0.8,
        )
        own.append((own1, own2))
    last = []
    for i, (_, count) in enumerate(CHUNKS):
        send = call(
            functools.partial(second_body, count),
            [pltpu.VMEM((count, ROWS, COLS), BF16)] * 2,
            (*own[i], *got[i]),
            [VMEM_SPEC] * 4,
            us=0.2,
        )
        last.append((swap(send[0], "mem", True), swap(send[1], "mem", False)))
    weighted, near = [], []
    for i, chunk in enumerate(CHUNKS):
        piece, terms = call(
            functools.partial(misfit_body, chunk, factor),
            [pltpu.VMEM((2 * chunk[1], ROWS, COLS), BF16), tile],
            (*own[i], *got[i], *last[i], inn, prec, terms),
            [VMEM_SPEC] * 9,
            us=0.3,
        )
        weighted.append(piece)
        near.append((swap(piece, "mem", False), swap(piece, "mem", True)))
    got_terms = trade(terms, ("lat",), (4, 5, 6, 7, 0, 1, 2, 3))
    (acc,) = call(
        own_pull_body,
        [pltpu.VMEM(block, F32)],
        (sel0, sel1, *weighted),
        [VMEM_SPEC] * (2 + len(CHUNKS)),
        us=0.6,
    )
    far = []
    for i, chunk in enumerate(CHUNKS):
        last_one = i == len(CHUNKS) - 1
        near[i], acc, got_terms = lax.optimization_barrier((near[i], acc, got_terms))
        a, b = near[i]
        far.append((swap(b[: chunk[1]], "mem", False), swap(a[chunk[1] :], "mem", True)))
        terms = terms + got_terms
        if last_one:
            got_terms = trade(terms, ("lat", "lon"), [lat * 4 + (lon ^ 2) for lat in range(8) for lon in range(4)])
        else:
            got_terms = trade(terms, ("lat",), (3, 2, 1, 0, 7, 6, 5, 4))
        (acc,) = call(
            functools.partial(near_pull_body, chunk),
            [pltpu.VMEM(block, F32)],
            (sel0, sel1, acc, a, b),
            [VMEM_SPEC] * 5,
            us=0.4,
        )
    source, terms = call(
        functools.partial(far_pull_body, factor),
        [pltpu.VMEM((MEMBERS + 1, ROWS, COLS), F32), tile],
        (sel0, sel1, acc, loc_norm, terms, got_terms, *[f for pair in far for f in pair]),
        [VMEM_SPEC] * (6 + 2 * len(CHUNKS)),
        us=0.6,
    )
    even, odd = swap(source, "lat", False), swap(source, "lat", True)
    got = (
        swap(terms, "mem", False),
        trade(terms, ("mem", "lat"), [(mem ^ 1) * 8 + (lat ^ 1) for mem in range(4) for lat in range(8)]),
    )
    even, odd, got = lax.optimization_barrier((even, odd, got))
    ext, packed, terms = pack(MEMBERS, False, source, even, odd, (terms, *got))
    even, odd = swap(packed, "lon", False), swap(packed, "lon", True)
    got = (
        trade(terms, ("lon",), (1, 0, 3, 2)),
        swap(terms, "mem", True),
        trade(terms, ("mem", "lon"), [(3 - mem) * 4 + (lon ^ 1) for mem in range(4) for lon in range(4)]),
    )
    even, odd, got = lax.optimization_barrier((even, odd, got))
    gradient, cost = call(
        functools.partial(adjoint_body, 0.5 / cells),
        [jax.ShapeDtypeStruct(block, F32), jax.ShapeDtypeStruct((1, COLS), F32)],
        (ext, even, odd, rate, control, terms, *got),
        [VMEM_SPEC] * 9,
        us=1.5,
    )
    return gradient, cost[0, 0]


def solution(mesh):
    return jax.shard_map(
        on_device,
        mesh=mesh,
        in_specs=(
            P("mem", "lat", "lon"),
            P("mem", None, None, None, "lat", "lon"),
            P("lat", "lon"),
            P("lat", "lon"),
            P(None, None, "lat", "lon"),
            P(None, None, "lat", "lon"),
            P("lat", "lon"),
        ),
        out_specs=(P("mem", "lat", "lon"), P()),
        check_vma=False,
    )
```

```python
import functools
import math

import jax
import jax.numpy as jnp
from jax import lax
from jax.experimental import pallas as pl
from jax.experimental.pallas import tpu as pltpu
from jax.sharding import PartitionSpec as P

F32 = jnp.float32
BF16 = jnp.bfloat16
PASSES = 10
REACH = 10
ROWS, COLS = 16, 128
MEMBERS = 5
PLANES = 280
SHARE = PLANES // 4
CHUNKS = ((0, 35), (35, 35))
PARTNERS = (2, 1, 3)
MIB = 1 << 20

VMEM_SPEC = pl.BlockSpec(memory_space=pltpu.VMEM)
ANY_SPEC = pl.BlockSpec(memory_space=pl.ANY)


def call(body, outs, args, specs, scratch=(), limit=8 * MIB, us=1.0, aliases=None):
    def placed(*refs):
        body([lax.axis_index(a) for a in ("mem", "lat", "lon")], *refs)

    return pl.pallas_call(
        placed,
        out_shape=outs,
        in_specs=specs,
        out_specs=[VMEM_SPEC] * len(outs),
        scratch_shapes=list(scratch),
        input_output_aliases=aliases or {},
        compiler_params=pltpu.CompilerParams(vmem_limit_bytes=limit),
        cost_estimate=pl.CostEstimate(
            flops=int(us * 1e6), bytes_accessed=int(us * 3e6), transcendentals=0
        ),
    )(*args)


def in_hbm(cells):
    return pltpu.with_memory_space_constraint(cells, pltpu.HBM)


def swap(cells, axis, odd):
    count = lax.axis_size(axis)
    pairs = []
    for i in range(count):
        to = i ^ 1 if not odd else ((i + 1) ^ 1) - 1
        pairs.append((i, to % count))
    return lax.ppermute(cells, axis, pairs)


def trade(cells, axes, to):
    return lax.ppermute(cells, axes, list(enumerate(to)))


def share(cells, partner):
    return trade(cells, ("mem",), [i ^ partner for i in range(4)])


def pack_body(fields, mask_edges, ids, own, even, odd, *rest):
    if len(rest) > 2:
        terms, got, ext, packed, new_terms = rest
        summed = (terms[...] + even[fields, :8]) + (got[...] + odd[fields, :8])
        new_terms[...] = summed
        packed[3 * ROWS :] = summed
    else:
        ext, packed = rest
    lat = ids[1]
    is_even = lax.rem(lat, 2) == 0
    lane = lax.broadcasted_iota(jnp.int32, (3 * ROWS, COLS), 1)
    out = jnp.zeros((3 * ROWS, COLS), F32)
    for f in range(fields):
        a, b = even[f], odd[f]
        up = jnp.where(is_even, b, a)
        down = jnp.where(is_even, a, b)
        if mask_edges:
            up = jnp.where(lat == 0, 0.0, up)
            down = jnp.where(lat == 7, 0.0, down)
        whole = jnp.concatenate([up, own[f], down], axis=0)
        ext[f] = whole
        at = 2 * REACH * f
        turned = pltpu.roll(whole, (at + REACH) % COLS, 1)
        out = jnp.where((lane >= at) & (lane < at + 2 * REACH), turned, out)
    packed[: 3 * ROWS] = out


def pack(fields, mask_edges, own, even, odd, terms=()):
    return call(
        functools.partial(pack_body, fields, mask_edges),
        [pltpu.VMEM((fields, 3 * ROWS, COLS), F32), pltpu.VMEM((3 * ROWS + (8 if terms else 0), COLS), F32)]
        + [pltpu.VMEM((8, COLS), F32)] * (1 if terms else 0),
        (own, even, odd, *terms),
        [VMEM_SPEC] * (3 + len(terms)),
        us=0.3,
    )


def group(lane, m):
    return (lane >= 2 * REACH * m) & (lane < 2 * REACH * (m + 1))


def halo_of(fields, ids, even, odd):
    is_even = lax.rem(ids[2], 2) == 0
    lane = lax.broadcasted_iota(jnp.int32, (3 * ROWS, COLS), 1)
    west = lane < 0
    for f in range(fields):
        at = 2 * REACH * f
        west = west | ((lane >= at) & (lane < at + REACH))
    a, b = even[: 3 * ROWS], odd[: 3 * ROWS]
    return jnp.where(west, jnp.where(is_even, b, a), jnp.where(is_even, a, b))


def lap(own, side):
    rows = side.shape[0]
    lane = lax.broadcasted_iota(jnp.int32, side.shape, 1)

    def total(v, west, east):
        above = pltpu.roll(v, 1, 0)
        below = pltpu.roll(v, rows - 1, 0)
        return (above + below) + (west + east) - 4.0 * v

    west_side, east_side = pltpu.roll(side, 1, 1), pltpu.roll(side, COLS - 1, 1)
    out = []
    for m in range(MEMBERS):
        at = 2 * REACH * m + REACH
        v = own[m]
        west = jnp.where(lane == 0, pltpu.roll(side, COLS - at + 1, 1), pltpu.roll(v, 1, 1))
        east = jnp.where(lane == COLS - 1, pltpu.roll(side, COLS - at - 1, 1), pltpu.roll(v, COLS - 1, 1))
        out.append(total(v, west, east))
        west_side = jnp.where(lane == at, pltpu.roll(v, at + 1, 1), west_side)
        east_side = jnp.where(lane == at - 1, pltpu.roll(v, at - 1, 1), east_side)
    return out, total(side, west_side, east_side)


def forward_pass(state, rate):
    (own, side), (rate_own, rate_side) = state, rate
    a, b = lap(own, side)
    return [v + rate_own * x for v, x in zip(own, a)], side + rate_side * b


def adjoint_pass(state, rate):
    (own, side), (rate_own, rate_side) = state, rate
    a, b = lap([rate_own * v for v in own], rate_side * side)
    return [v + x for v, x in zip(own, a)], side + b


def sweep(step, own, side, rate):
    cut = ROWS // 2
    state = (own, side)
    for _ in range(2):
        state = step(state, rate)
    own, side = [v[cut:-cut] for v in state[0]], state[1][cut:-cut]
    rate = tuple(v[cut:-cut] for v in rate)
    own, side = lax.fori_loop(0, PASSES - 2, lambda _, s: step(s, rate), (own, side))
    return [v[ROWS - cut : -(ROWS - cut)] for v in own]


def partner_of(mem, partner):
    return mem + partner - 2 * (lax.rem(mem, 2) * (partner % 2)) - 4 * (lax.div(mem, 2) * (partner // 2))


def select_body(partners, own, ids, anomalies, obs_time, *rest):
    if own:
        innovation, precision, sel, inn_own, prec_own, buf, when, sems, own_sems = rest
        own = ((innovation, inn_own), (precision, prec_own))
    else:
        sel, buf, when, sems, own_sems = rest
        own = ()
    time_copy = pltpu.make_async_copy(obs_time, when, own_sems.at[2])
    time_copy.start()
    copies = []
    for g, partner in enumerate(partners):
        at = pl.ds(SHARE * partner_of(ids[0], partner), SHARE)
        for m in range(MEMBERS):
            copy = pltpu.make_async_copy(anomalies.at[m, :, at], buf.at[g, m], sems.at[g * MEMBERS + m])
            copy.start()
            copies.append(copy)
    own_copies = []
    for k, (src, dst) in enumerate(own):
        copy = pltpu.make_async_copy(src.at[pl.ds(SHARE * ids[0], SHARE)], dst, own_sems.at[k])
        copy.start()
        own_copies.append(copy)
    time_copy.wait()
    at_zero = when[...].astype(F32).astype(BF16) == 0
    for n, copy in enumerate(copies):
        g, m = divmod(n, MEMBERS)
        copy.wait()

        def plane(r, c, g=g, m=m):
            sel[g, m, r] = jnp.where(at_zero, buf[g, m, 0, r], buf[g, m, 1, r])
            return c

        lax.fori_loop(0, SHARE, plane, 0, unroll=7)
    for copy in own_copies:
        copy.wait()


def select(partners, anomalies, obs_time, own=()):
    count = len(partners)
    return call(
        functools.partial(select_body, partners, bool(own)),
        [pltpu.VMEM((count, MEMBERS, SHARE, ROWS, COLS), BF16)]
        + [pltpu.VMEM((SHARE, ROWS, COLS), F32)] * (2 if own else 0),
        (anomalies, obs_time, *own),
        [ANY_SPEC, ANY_SPEC] + ([ANY_SPEC, ANY_SPEC] if own else []),
        scratch=[
            pltpu.VMEM((count, MEMBERS, 2, SHARE, ROWS, COLS), BF16),
            pltpu.VMEM((ROWS, COLS), jnp.int32),
            pltpu.SemaphoreType.DMA((count * MEMBERS,)),
            pltpu.SemaphoreType.DMA((3,)),
        ],
        limit=16 * MIB,
        us=2.5,
    )


def share_sums(chunk, sel, w, dtype, out):
    first, count = chunk
    ws = [w[m] for m in range(MEMBERS)]

    def plane(r, c):
        total = sel[0, first + r].astype(F32) * ws[0]
        for m in range(1, MEMBERS):
            total = total + sel[m, first + r].astype(F32) * ws[m]
        out[r] = total.astype(dtype)
        return c

    lax.fori_loop(0, count, plane, 0, unroll=5 if count % 5 == 0 else 1)


def sends_body(chunk, ids, sent1, sent2, w, *outs):
    for sel, out in zip((sent1.at[0], sent1.at[1], sent2.at[0]), outs):
        share_sums(chunk, sel, w, BF16, out)


def stays_body(ids, kept, w, own):
    share_sums((0, SHARE), kept.at[0], w, F32, own)


def forward_body(chunk, ids, ext, even, odd, loc_norm, sent1, sent2, w, rate, terms, *sends):
    halo = halo_of(MEMBERS + 1, ids, even, odd)
    lane = lax.broadcasted_iota(jnp.int32, (3 * ROWS, COLS), 1)
    side = jnp.where(lane < 2 * REACH * MEMBERS, halo, 0.0)
    rate_side = jnp.zeros((3 * ROWS, COLS), F32)
    for m in range(MEMBERS):
        turned = pltpu.roll(halo, (COLS - 2 * REACH * (MEMBERS - m)) % COLS, 1)
        rate_side = jnp.where(group(lane, m), turned, rate_side)
    rate[0] = ext[MEMBERS]
    rate[1] = rate_side
    squares = jnp.zeros((ROWS, COLS), F32)
    for m in range(MEMBERS):
        mine = ext[m, ROWS : 2 * ROWS]
        squares = squares + mine * mine
    terms[...] = squares[:8] + squares[8:]
    spread = sweep(forward_pass, [ext[m] for m in range(MEMBERS)], side, (ext[MEMBERS], rate_side))
    for m in range(MEMBERS):
        w[m] = (loc_norm[...] * spread[m]).astype(BF16).astype(F32)
    sends_body(chunk, ids, sent1, sent2, w, *sends)


def rides(chunk):
    return 1 if chunk == CHUNKS[-1] else 0


def ridden(plane):
    plane = plane.astype(F32)
    return plane[:8] + plane[8:]


def misfit_body(chunk, factor, ids, own, got1, got2, got3, inn, prec, terms, weighted, new_terms):
    first, count = chunk

    def plane(r, c):
        sums = (own[first + r] + got1[r].astype(F32)) + (got2[r].astype(F32) + got3[r].astype(F32))
        misfit = factor * sums - inn[first + r]
        scaled = prec[first + r] * misfit
        weighted[r] = scaled.astype(BF16)
        return c + misfit * scaled

    total = lax.fori_loop(0, count, plane, jnp.zeros((ROWS, COLS), F32), unroll=5 if count % 5 == 0 else 1)
    summed = terms[...] + (total[:8] + total[8:])
    new_terms[...] = summed
    if rides(chunk):
        high = summed.astype(BF16).astype(F32)
        weighted[count] = jnp.concatenate([high, summed - high], axis=0).astype(BF16)


def pull(sel, chunk, ref, acc):
    first, count = chunk

    def plane(r, acc):
        x = ref[r].astype(F32)
        return tuple(acc[m] + sel[m, first + r].astype(F32) * x for m in range(MEMBERS))

    return lax.fori_loop(0, count, plane, acc, unroll=5 if count % 5 == 0 else 1)


def own_pull_body(ids, kept, *rest):
    refs, new = rest[:-1], rest[-1]
    acc = tuple(jnp.zeros((ROWS, COLS), F32) for _ in range(MEMBERS))
    for chunk, ref in zip(CHUNKS, refs):
        acc = pull(kept.at[0], chunk, ref, acc)
    for m in range(MEMBERS):
        new[m] = acc[m]


def pull_all(chunk, sent1, sent2, old, refs):
    acc = tuple(old[m] for m in range(MEMBERS))
    for sel, ref in zip((sent1.at[0], sent1.at[1], sent2.at[0]), refs):
        acc = pull(sel, chunk, ref, acc)
    return acc


RELAYED = 20


def pull_body(chunk, ids, sent1, sent2, old, ref1, ref2, ref3, ref4, new):
    first, count = chunk
    acc = tuple(old[m] for m in range(MEMBERS))
    acc = pull(sent1.at[0], (first, RELAYED), ref1, acc)
    acc = pull(sent1.at[0], (first + RELAYED, count - RELAYED), ref2, acc)
    acc = pull(sent1.at[1], chunk, ref3, acc)
    acc = pull(sent2.at[0], chunk, ref4, acc)
    for m in range(MEMBERS):
        new[m] = acc[m]


def last_pull_body(factor, ids, sent1, sent2, old, ref1, ref2, ref3, loc_norm, mine, new, terms):
    acc = pull_all(CHUNKS[-1], sent1, sent2, old, (ref1, ref2, ref3))
    for m in range(MEMBERS):
        new[m] = loc_norm[...] * (factor * acc[m])
    at = CHUNKS[-1][1]
    summed = (ridden(mine[at]) + ridden(ref2[at])) + (ridden(ref3[at]) + ridden(ref1[at]))
    row = lax.broadcasted_iota(jnp.int32, (8, COLS), 0)
    summed = jnp.where(row == ids[1], jnp.sum(summed, axis=0, keepdims=True), 0.0)
    terms[...] = summed
    new[MEMBERS, :8] = summed
    new[MEMBERS, 8:] = jnp.zeros((ROWS - 8, COLS), F32)


def pass_body(ids, odd, passed):
    passed[...] = odd[3 * ROWS :]


def cost_body(ids, terms, even, passed, got, summed):
    summed[...] = (terms[...] + even[3 * ROWS :]) + (passed[...] + got[...])


def last_cost_body(scale, ids, summed, got, cost):
    cost[...] = jnp.broadcast_to(jnp.sum(summed[...] + got[...]) * scale, (1, COLS))


def adjoint_body(ids, ext, even, odd, rate, control, out):
    side = halo_of(MEMBERS, ids, even, odd)
    back = sweep(adjoint_pass, [ext[m] for m in range(MEMBERS)], side, (rate[0], rate[1]))
    for m in range(MEMBERS):
        out[m] = control[m] + back[m]


def on_device(control, anomalies, diffusivity, loc_norm, innovation, obs_precision, obs_time):
    members = MEMBERS * lax.axis_size("mem")
    cells = members * ROWS * COLS * lax.axis_size("lat") * lax.axis_size("lon")
    factor = 1.0 / math.sqrt(members - 1)
    obs_time = in_hbm(obs_time)
    anomalies = in_hbm(anomalies.reshape(MEMBERS, 2, PLANES, ROWS, COLS))
    innovation = in_hbm(innovation.reshape(PLANES, ROWS, COLS))
    obs_precision = in_hbm(obs_precision.reshape(PLANES, ROWS, COLS))
    block = (MEMBERS, ROWS, COLS)

    fields = jnp.concatenate([control, diffusivity[None]], axis=0)
    even, odd = swap(fields, "lat", False), swap(fields, "lat", True)
    (sent1,) = select(PARTNERS[:2], anomalies, obs_time)
    even, odd, sent1 = lax.optimization_barrier((even, odd, sent1))
    ext, packed = pack(MEMBERS + 1, True, fields, even, odd)
    even, odd = swap(packed, "lon", False), swap(packed, "lon", True)
    (sent2,) = select(PARTNERS[2:], anomalies, obs_time)
    even, odd, sent2 = lax.optimization_barrier((even, odd, sent2))

    def blocks(count):
        return [pltpu.VMEM((count, ROWS, COLS), BF16)] * 3

    tile = pltpu.VMEM((8, COLS), F32)
    w, rate, terms, *send = call(
        functools.partial(forward_body, CHUNKS[0]),
        [pltpu.VMEM(block, F32), pltpu.VMEM((2, 3 * ROWS, COLS), F32), tile, *blocks(CHUNKS[0][1])],
        (ext, even, odd, loc_norm, sent1, sent2),
        [VMEM_SPEC] * 6,
        us=2.0,
    )
    got = []
    for i, chunk in enumerate(CHUNKS):
        if i > 0:
            send = call(
                functools.partial(sends_body, chunk), blocks(chunk[1]), (sent1, sent2, w), [VMEM_SPEC] * 3, us=0.3
            )
        got.append([share(cells, p) for cells, p in zip(send, PARTNERS)])
    kept, inn, prec = select((0,), anomalies, obs_time, (innovation, obs_precision))
    (own,) = call(stays_body, [pltpu.VMEM((SHARE, ROWS, COLS), F32)], (kept, w), [VMEM_SPEC] * 2, us=0.3)
    weighted, near = [], []
    for i, chunk in enumerate(CHUNKS):
        piece, terms = call(
            functools.partial(misfit_body, chunk, factor),
            [pltpu.VMEM((chunk[1] + rides(chunk), ROWS, COLS), BF16), tile],
            (own, *got[i], inn, prec, terms),
            [VMEM_SPEC] * 7,
            us=0.3,
        )
        weighted.append(piece)
        if i == len(CHUNKS) - 1:
            near.append([share(piece, p) for p in PARTNERS])
        else:
            a, b = share(piece, 1), share(piece, 3)
            near.append([share(b[:RELAYED], 1), share(a[RELAYED:], 3), a, b])
    (acc,) = call(
        own_pull_body,
        [pltpu.VMEM(block, F32)],
        (kept, *weighted),
        [VMEM_SPEC] * (1 + len(CHUNKS)),
        us=0.4,
    )
    for i, chunk in enumerate(CHUNKS[:-1]):
        (acc,) = call(
            functools.partial(pull_body, chunk),
            [pltpu.VMEM(block, F32)],
            (sent1, sent2, acc, *near[i]),
            [VMEM_SPEC] * 7,
            us=0.5,
        )
    source, terms = call(
        functools.partial(last_pull_body, factor),
        [pltpu.VMEM((MEMBERS + 1, ROWS, COLS), F32), tile],
        (sent1, sent2, acc, *near[-1], loc_norm, weighted[-1]),
        [VMEM_SPEC] * 8,
        us=0.5,
    )
    even, odd = swap(source, "lat", False), swap(source, "lat", True)
    got = trade(terms, ("lat",), (2, 3, 0, 1, 6, 7, 4, 5))
    even, odd, got = lax.optimization_barrier((even, odd, got))
    ext, packed, terms = pack(MEMBERS, False, source, even, odd, (terms, got))
    even, odd = swap(packed, "lon", False), swap(packed, "lon", True)
    (passed,) = call(pass_body, [tile], (odd,), [VMEM_SPEC], us=0.1)
    got = swap(passed, "lon", False)
    (terms,) = call(cost_body, [tile], (terms, even, passed, got), [VMEM_SPEC] * 4, us=0.1)
    got = trade(terms, ("lat",), (4, 5, 6, 7, 0, 1, 2, 3))
    even, odd, terms = lax.optimization_barrier((even, odd, terms))
    (gradient,) = call(
        adjoint_body,
        [jax.ShapeDtypeStruct(block, F32)],
        (ext, even, odd, rate, control),
        [VMEM_SPEC] * 5,
        us=3.0,
    )
    (cost,) = call(
        functools.partial(last_cost_body, 0.5 / cells),
        [jax.ShapeDtypeStruct((1, COLS), F32)],
        (terms, got),
        [VMEM_SPEC] * 2,
        us=0.1,
    )
    return gradient, cost[0, 0]


def solution(mesh):
    return jax.shard_map(
        on_device,
        mesh=mesh,
        in_specs=(
            P("mem", "lat", "lon"),
            P("mem", None, None, None, "lat", "lon"),
            P("lat", "lon"),
            P("lat", "lon"),
            P(None, None, "lat", "lon"),
            P(None, None, "lat", "lon"),
            P("lat", "lon"),
        ),
        out_specs=(P("mem", "lat", "lon"), P()),
        check_vma=False,
    )
```

```python
import functools
import math

import jax
import jax.numpy as jnp
from jax import lax
from jax.experimental import pallas as pl
from jax.experimental.pallas import tpu as pltpu
from jax.sharding import PartitionSpec as P

F32 = jnp.float32
BF16 = jnp.bfloat16
PASSES = 10
REACH = 10
ROWS, COLS = 16, 128
MEMBERS = 5
PLANES = 280
SHARE = PLANES // 4
CHUNKS = ((0, 35), (35, 35))
PARTNERS = (2, 1, 3)
MIB = 1 << 20

VMEM_SPEC = pl.BlockSpec(memory_space=pltpu.VMEM)
ANY_SPEC = pl.BlockSpec(memory_space=pl.ANY)


def call(body, outs, args, specs, scratch=(), limit=8 * MIB, us=1.0, aliases=None):
    def placed(*refs):
        body([lax.axis_index(a) for a in ("mem", "lat", "lon")], *refs)

    return pl.pallas_call(
        placed,
        out_shape=outs,
        in_specs=specs,
        out_specs=[VMEM_SPEC] * len(outs),
        scratch_shapes=list(scratch),
        input_output_aliases=aliases or {},
        compiler_params=pltpu.CompilerParams(vmem_limit_bytes=limit),
        cost_estimate=pl.CostEstimate(
            flops=int(us * 1e6), bytes_accessed=int(us * 3e6), transcendentals=0
        ),
    )(*args)


def in_hbm(cells):
    return pltpu.with_memory_space_constraint(cells, pltpu.HBM)


def swap(cells, axis, odd):
    count = lax.axis_size(axis)
    pairs = []
    for i in range(count):
        to = i ^ 1 if not odd else ((i + 1) ^ 1) - 1
        pairs.append((i, to % count))
    return lax.ppermute(cells, axis, pairs)


def trade(cells, axes, to):
    return lax.ppermute(cells, axes, list(enumerate(to)))


def share(cells, partner):
    return trade(cells, ("mem",), [i ^ partner for i in range(4)])


SUB = 8
TALL = 3 * ROWS
TILES = (TALL * SUB, COLS)


def put(ref, f, rows):
    ref[pl.ds(f, TALL, stride=SUB)] = rows


def pack_body(fields, first, ids, own, even, odd, *rest):
    if first:
        ext, rate, packed = rest
    else:
        terms, ext, packed, new_terms = rest
        new_terms[...] = (terms[...] + even[fields, :8]) + odd[fields, :8]
    lat = ids[1]
    is_even = lax.rem(lat, 2) == 0
    lane = lax.broadcasted_iota(jnp.int32, (TALL, COLS), 1)
    out = jnp.zeros((TALL, COLS), F32)
    for f in range(fields):
        a, b = even[f], odd[f]
        up = jnp.where(is_even, b, a)
        down = jnp.where(is_even, a, b)
        if first:
            up = jnp.where(lat == 0, 0.0, up)
            down = jnp.where(lat == 7, 0.0, down)
        whole = jnp.concatenate([up, own[f], down], axis=0)
        if f < MEMBERS:
            put(ext, f, whole)
        else:
            for sub in range(SUB):
                put(rate, sub, whole)
        at = 2 * REACH * f
        turned = pltpu.roll(whole, (at + REACH) % COLS, 1)
        out = jnp.where((lane >= at) & (lane < at + 2 * REACH), turned, out)
    packed[:TALL] = out


def pack(fields, own, even, odd, terms=()):
    return call(
        functools.partial(pack_body, fields, not terms),
        [pltpu.VMEM(TILES, F32)] * (1 if terms else 2)
        + [pltpu.VMEM((TALL + (8 if terms else 0), COLS), F32)]
        + [pltpu.VMEM((8, COLS), F32)] * len(terms),
        (own, even, odd, *terms),
        [VMEM_SPEC] * (3 + len(terms)),
        us=0.3,
    )


def ride_body(ids, held, terms, got, packed, new_terms):
    summed = terms[...] + got[...]
    new_terms[...] = summed
    packed[TALL:] = summed


def halo_of(fields, ids, even, odd):
    is_even = lax.rem(ids[2], 2) == 0
    lane = lax.broadcasted_iota(jnp.int32, (TALL, COLS), 1)
    west = lane < 0
    for f in range(fields):
        at = 2 * REACH * f
        west = west | ((lane >= at) & (lane < at + REACH))
    a, b = even[:TALL], odd[:TALL]
    return jnp.where(west, jnp.where(is_even, b, a), jnp.where(is_even, a, b))


def spread_halo(halo, f):
    return pltpu.roll(halo, (2 * COLS - REACH - 2 * REACH * f) % COLS, 1)


def sweep(adjoint, ext, side, rate):
    lane = lax.broadcasted_iota(jnp.int32, (SUB, COLS), 1)
    first, last = lane == 0, lane == COLS - 1
    low = ROWS - REACH

    def tile(row):
        return pl.ds(SUB * row, SUB)

    own = [ext[tile(low + r)] for r in range(ROWS + 2 * REACH)]
    halo = [side[tile(low + r)] for r in range(ROWS + 2 * REACH)]
    for _ in range(PASSES):
        count = len(own)
        rate_own = [rate[0, tile(low + r)] for r in range(count)]
        rate_halo = [rate[1, tile(low + r)] for r in range(count)]
        if adjoint:
            a = [v * d for v, d in zip(own, rate_own)]
            b = [v * d for v, d in zip(halo, rate_halo)]
        else:
            a, b = own, halo
        new_own, new_halo = [], []
        for r in range(1, count - 1):
            a_west, b_west = pltpu.roll(a[r], 1, 1), pltpu.roll(b[r], 1, 1)
            a_east, b_east = pltpu.roll(a[r], COLS - 1, 1), pltpu.roll(b[r], COLS - 1, 1)
            beside_a = jnp.where(first, b_west, a_west) + jnp.where(last, b_east, a_east)
            beside_b = jnp.where(first, a_west, b_west) + jnp.where(last, a_east, b_east)
            lap_a = (a[r - 1] + a[r + 1]) + beside_a - 4.0 * a[r]
            lap_b = (b[r - 1] + b[r + 1]) + beside_b - 4.0 * b[r]
            if not adjoint:
                lap_a, lap_b = rate_own[r] * lap_a, rate_halo[r] * lap_b
            new_own.append(own[r] + lap_a)
            new_halo.append(halo[r] + lap_b)
        own, halo = new_own, new_halo
        low += 1
    return own


def members_of(tiles, room):
    for r, tile in enumerate(tiles):
        room[pl.ds(SUB * r, SUB)] = tile
    return [room[pl.ds(m, ROWS, stride=SUB)] for m in range(MEMBERS)]


def partner_of(mem, partner):
    return mem + partner - 2 * (lax.rem(mem, 2) * (partner % 2)) - 4 * (lax.div(mem, 2) * (partner // 2))


def select_body(partners, own, ids, anomalies, obs_time, *rest):
    if own:
        innovation, precision, sel, inn_own, prec_own, buf, when, sems, own_sems = rest
        own = ((innovation, inn_own), (precision, prec_own))
    else:
        sel, buf, when, sems, own_sems = rest
        own = ()
    time_copy = pltpu.make_async_copy(obs_time, when, own_sems.at[2])
    time_copy.start()
    copies = []
    for g, partner in enumerate(partners):
        at = pl.ds(SHARE * partner_of(ids[0], partner), SHARE)
        for m in range(MEMBERS):
            copy = pltpu.make_async_copy(anomalies.at[m, :, at], buf.at[g, m], sems.at[g * MEMBERS + m])
            copy.start()
            copies.append(copy)
    own_copies = []
    for k, (src, dst) in enumerate(own):
        copy = pltpu.make_async_copy(src.at[pl.ds(SHARE * ids[0], SHARE)], dst, own_sems.at[k])
        copy.start()
        own_copies.append(copy)
    time_copy.wait()
    at_zero = when[...].astype(F32).astype(BF16) == 0
    for n, copy in enumerate(copies):
        g, m = divmod(n, MEMBERS)
        copy.wait()

        def plane(r, c, g=g, m=m):
            sel[g, m, r] = jnp.where(at_zero, buf[g, m, 0, r], buf[g, m, 1, r])
            return c

        lax.fori_loop(0, SHARE, plane, 0, unroll=7)
    for copy in own_copies:
        copy.wait()


def select(partners, anomalies, obs_time, own=()):
    count = len(partners)
    return call(
        functools.partial(select_body, partners, bool(own)),
        [pltpu.VMEM((count, MEMBERS, SHARE, ROWS, COLS), BF16)]
        + [pltpu.VMEM((SHARE, ROWS, COLS), F32)] * (2 if own else 0),
        (anomalies, obs_time, *own),
        [ANY_SPEC, ANY_SPEC] + ([ANY_SPEC, ANY_SPEC] if own else []),
        scratch=[
            pltpu.VMEM((count, MEMBERS, 2, SHARE, ROWS, COLS), BF16),
            pltpu.VMEM((ROWS, COLS), jnp.int32),
            pltpu.SemaphoreType.DMA((count * MEMBERS,)),
            pltpu.SemaphoreType.DMA((3,)),
        ],
        limit=16 * MIB,
        us=2.5,
    )


def share_sums(chunk, sel, w, dtype, out):
    first, count = chunk
    ws = [w[m] for m in range(MEMBERS)]

    def plane(r, c):
        total = sel[0, first + r].astype(F32) * ws[0]
        for m in range(1, MEMBERS):
            total = total + sel[m, first + r].astype(F32) * ws[m]
        out[r] = total.astype(dtype)
        return c

    lax.fori_loop(0, count, plane, 0, unroll=5 if count % 5 == 0 else 1)


def sends_body(chunk, ids, sent1, sent2, w, *outs):
    for sel, out in zip((sent1.at[0], sent1.at[1], sent2.at[0]), outs):
        share_sums(chunk, sel, w, BF16, out)


def stays_body(ids, kept, w, own):
    share_sums((0, SHARE), kept.at[0], w, F32, own)


def forward_body(chunk, ids, ext, rate_own, own, even, odd, loc_norm, sent1, sent2, w, rate, terms, *rest):
    sends, side, room = rest[:-2], rest[-2], rest[-1]
    halo = halo_of(MEMBERS + 1, ids, even, odd)
    lane = lax.broadcasted_iota(jnp.int32, (TALL, COLS), 1)
    near = (lane < REACH) | (lane >= COLS - REACH)
    rate_side = jnp.where(near, spread_halo(halo, MEMBERS), 0.0)
    rate[0] = rate_own[...]
    for sub in range(SUB):
        put(rate.at[1], sub, rate_side)
    for m in range(MEMBERS):
        put(side, m, spread_halo(halo, m))
    squares = jnp.zeros((ROWS, COLS), F32)
    for m in range(MEMBERS):
        squares = squares + own[m] * own[m]
    terms[...] = squares[:8] + squares[8:]
    for m, spread in enumerate(members_of(sweep(False, ext, side, rate), room)):
        w[m] = (loc_norm[...] * spread).astype(BF16).astype(F32)
    sends_body(chunk, ids, sent1, sent2, w, *sends)


def rides(chunk):
    return 1 if chunk == CHUNKS[-1] else 0


def ridden(plane):
    plane = plane.astype(F32)
    return plane[:8] + plane[8:]


def misfit_body(chunk, factor, ids, own, got1, got2, got3, inn, prec, terms, weighted, *new_terms):
    first, count = chunk

    def plane(r, c):
        sums = (own[first + r] + got1[r].astype(F32)) + (got2[r].astype(F32) + got3[r].astype(F32))
        misfit = factor * sums - inn[first + r]
        scaled = prec[first + r] * misfit
        weighted[r] = scaled.astype(BF16)
        return c + misfit * scaled

    total = lax.fori_loop(0, count, plane, jnp.zeros((ROWS, COLS), F32), unroll=5 if count % 5 == 0 else 1)
    summed = terms[...] + (total[:8] + total[8:])
    if not rides(chunk):
        new_terms[0][...] = summed
    else:
        high = summed.astype(BF16).astype(F32)
        weighted[count] = jnp.concatenate([high, summed - high], axis=0).astype(BF16)


def pull(sel, chunk, ref, acc):
    first, count = chunk

    def plane(r, acc):
        x = ref[r].astype(F32)
        return tuple(acc[m] + sel[m, first + r].astype(F32) * x for m in range(MEMBERS))

    return lax.fori_loop(0, count, plane, acc, unroll=5 if count % 5 == 0 else 1)


def own_pull_body(ids, kept, *rest):
    refs, new = rest[:-1], rest[-1]
    acc = tuple(jnp.zeros((ROWS, COLS), F32) for _ in range(MEMBERS))
    for chunk, ref in zip(CHUNKS, refs):
        acc = pull(kept.at[0], chunk, ref, acc)
    for m in range(MEMBERS):
        new[m] = acc[m]


def pull_all(chunk, sent1, sent2, old, refs):
    acc = tuple(old[m] for m in range(MEMBERS))
    for sel, ref in zip((sent1.at[0], sent1.at[1], sent2.at[0]), refs):
        acc = pull(sel, chunk, ref, acc)
    return acc


RELAYED = 20


def pull_body(chunk, ids, sent1, sent2, old, ref1, ref2, ref3, ref4, new):
    first, count = chunk
    acc = tuple(old[m] for m in range(MEMBERS))
    acc = pull(sent1.at[0], (first, RELAYED), ref1, acc)
    acc = pull(sent1.at[0], (first + RELAYED, count - RELAYED), ref2, acc)
    acc = pull(sent1.at[1], chunk, ref3, acc)
    acc = pull(sent2.at[0], chunk, ref4, acc)
    for m in range(MEMBERS):
        new[m] = acc[m]


def last_pull_body(factor, ids, sent1, sent2, old, ref1, ref2, ref3, loc_norm, mine, new, terms):
    acc = pull_all(CHUNKS[-1], sent1, sent2, old, (ref1, ref2, ref3))
    for m in range(MEMBERS):
        new[m] = loc_norm[...] * (factor * acc[m])
    at = CHUNKS[-1][1]
    summed = (ridden(mine[at]) + ridden(ref2[at])) + (ridden(ref3[at]) + ridden(ref1[at]))
    row = lax.broadcasted_iota(jnp.int32, (8, COLS), 0)
    summed = jnp.where(row == ids[1], jnp.sum(summed, axis=0, keepdims=True), 0.0)
    terms[...] = summed
    new[MEMBERS, :8] = summed
    new[MEMBERS, 8:] = jnp.zeros((ROWS - 8, COLS), F32)


def pass_body(ids, terms, even, odd, pair, passed):
    pair[:8] = terms[...] + even[TALL:]
    pair[8:] = odd[TALL:]
    passed[...] = odd[TALL:]


def cost_body(scale, ids, pair, got, far_pair, far_got, cost):
    mine = pair[:8] + (pair[8:] + got[...])
    far = far_pair[:8] + (far_pair[8:] + far_got[...])
    cost[...] = jnp.broadcast_to(jnp.sum(mine + far) * scale, (1, COLS))


def adjoint_body(ids, ext, even, odd, rate, control, out, side, room):
    halo = halo_of(MEMBERS, ids, even, odd)
    for m in range(MEMBERS):
        put(side, m, spread_halo(halo, m))
    for m, back in enumerate(members_of(sweep(True, ext, side, rate), room)):
        out[m] = control[m] + back


def on_device(control, anomalies, diffusivity, loc_norm, innovation, obs_precision, obs_time):
    members = MEMBERS * lax.axis_size("mem")
    cells = members * ROWS * COLS * lax.axis_size("lat") * lax.axis_size("lon")
    factor = 1.0 / math.sqrt(members - 1)
    obs_time = in_hbm(obs_time)
    anomalies = in_hbm(anomalies.reshape(MEMBERS, 2, PLANES, ROWS, COLS))
    innovation = in_hbm(innovation.reshape(PLANES, ROWS, COLS))
    obs_precision = in_hbm(obs_precision.reshape(PLANES, ROWS, COLS))
    block = (MEMBERS, ROWS, COLS)

    fields = jnp.concatenate([control, diffusivity[None]], axis=0)
    even, odd = swap(fields, "lat", False), swap(fields, "lat", True)
    (sent1,) = select(PARTNERS[:2], anomalies, obs_time)
    even, odd, sent1 = lax.optimization_barrier((even, odd, sent1))
    ext, rate, packed = pack(MEMBERS + 1, fields, even, odd)
    even, odd = swap(packed, "lon", False), swap(packed, "lon", True)
    (sent2,) = select(PARTNERS[2:], anomalies, obs_time)
    even, odd, sent2 = lax.optimization_barrier((even, odd, sent2))

    def blocks(count):
        return [pltpu.VMEM((count, ROWS, COLS), BF16)] * 3

    tile = pltpu.VMEM((8, COLS), F32)
    w, rate, terms, *send = call(
        functools.partial(forward_body, CHUNKS[0]),
        [pltpu.VMEM(block, F32), pltpu.VMEM((2, *TILES), F32), tile, *blocks(CHUNKS[0][1])],
        (ext, rate, fields, even, odd, loc_norm, sent1, sent2),
        [VMEM_SPEC] * 8,
        scratch=[pltpu.VMEM(TILES, F32), pltpu.VMEM((ROWS * SUB, COLS), F32)],
        us=2.0,
    )
    got = []
    for i, chunk in enumerate(CHUNKS):
        if i > 0:
            send = call(
                functools.partial(sends_body, chunk), blocks(chunk[1]), (sent1, sent2, w), [VMEM_SPEC] * 3, us=0.3
            )
        got.append([share(cells, p) for cells, p in zip(send, PARTNERS)])
    kept, inn, prec = select((0,), anomalies, obs_time, (innovation, obs_precision))
    (own,) = call(stays_body, [pltpu.VMEM((SHARE, ROWS, COLS), F32)], (kept, w), [VMEM_SPEC] * 2, us=0.3)
    weighted, near = [], []
    for i, chunk in enumerate(CHUNKS):
        piece, *rest = call(
            functools.partial(misfit_body, chunk, factor),
            [pltpu.VMEM((chunk[1] + rides(chunk), ROWS, COLS), BF16)] + [tile] * (1 - rides(chunk)),
            (own, *got[i], inn, prec, terms),
            [VMEM_SPEC] * 7,
            us=0.3,
        )
        terms = rest[0] if rest else None
        weighted.append(piece)
        if i == len(CHUNKS) - 1:
            near.append([share(piece, p) for p in PARTNERS])
        else:
            a, b = share(piece, 1), share(piece, 3)
            near.append([share(b[:RELAYED], 1), share(a[RELAYED:], 3), a, b])
    (acc,) = call(
        own_pull_body,
        [pltpu.VMEM(block, F32)],
        (kept, *weighted),
        [VMEM_SPEC] * (1 + len(CHUNKS)),
        us=0.4,
    )
    for i, chunk in enumerate(CHUNKS[:-1]):
        (acc,) = call(
            functools.partial(pull_body, chunk),
            [pltpu.VMEM(block, F32)],
            (sent1, sent2, acc, *near[i]),
            [VMEM_SPEC] * 7,
            us=0.5,
        )
    source, terms = call(
        functools.partial(last_pull_body, factor),
        [pltpu.VMEM((MEMBERS + 1, ROWS, COLS), F32), tile],
        (sent1, sent2, acc, *near[-1], loc_norm, weighted[-1]),
        [VMEM_SPEC] * 8,
        us=0.5,
    )
    even, odd = swap(source, "lat", False), swap(source, "lat", True)
    got = trade(terms, ("lat",), (2, 3, 0, 1, 6, 7, 4, 5))
    ext, packed, terms = pack(MEMBERS, source, even, odd, (terms,))
    packed, terms = call(
        ride_body,
        [pltpu.VMEM((TALL + 8, COLS), F32), tile],
        (packed, terms, got),
        [VMEM_SPEC] * 3,
        us=0.1,
        aliases={0: 0},
    )
    even, odd = swap(packed, "lon", False), swap(packed, "lon", True)
    pair, passed = call(
        pass_body, [pltpu.VMEM((16, COLS), F32), tile], (terms, even, odd), [VMEM_SPEC] * 3, us=0.1
    )
    got = swap(passed, "lon", False)
    far_pair = trade(pair, ("lat",), (4, 5, 6, 7, 0, 1, 2, 3))
    far_got = trade(passed, ("lat", "lon"), [(lat ^ 4) * 4 + (lon ^ 1) for lat in range(8) for lon in range(4)])
    even, odd, pair = lax.optimization_barrier((even, odd, pair))
    (gradient,) = call(
        adjoint_body,
        [jax.ShapeDtypeStruct(block, F32)],
        (ext, even, odd, rate, control),
        [VMEM_SPEC] * 5,
        scratch=[pltpu.VMEM(TILES, F32), pltpu.VMEM((ROWS * SUB, COLS), F32)],
        us=3.0,
    )
    (cost,) = call(
        functools.partial(cost_body, 0.5 / cells),
        [jax.ShapeDtypeStruct((1, COLS), F32)],
        (pair, got, far_pair, far_got),
        [VMEM_SPEC] * 4,
        us=0.1,
    )
    return gradient, cost[0, 0]


def solution(mesh):
    return jax.shard_map(
        on_device,
        mesh=mesh,
        in_specs=(
            P("mem", "lat", "lon"),
            P("mem", None, None, None, "lat", "lon"),
            P("lat", "lon"),
            P("lat", "lon"),
            P(None, None, "lat", "lon"),
            P(None, None, "lat", "lon"),
            P("lat", "lon"),
        ),
        out_specs=(P("mem", "lat", "lon"), P()),
        check_vma=False,
    )
```

```python
import functools
import math

import jax
import jax.numpy as jnp
from jax import lax
from jax.experimental import pallas as pl
from jax.experimental.pallas import tpu as pltpu
from jax.sharding import PartitionSpec as P

F32 = jnp.float32
BF16 = jnp.bfloat16
PASSES = 10
REACH = 10
ROWS, COLS = 16, 128
MEMBERS = 5
PLANES = 280
SHARE = PLANES // 4
CHUNKS = ((0, 40), (40, 30))
PARTNERS = (2, 1, 3)
MIB = 1 << 20

VMEM_SPEC = pl.BlockSpec(memory_space=pltpu.VMEM)
ANY_SPEC = pl.BlockSpec(memory_space=pl.ANY)


def call(body, outs, args, specs, scratch=(), limit=8 * MIB, us=1.0, aliases=None):
    def placed(*refs):
        body([lax.axis_index(a) for a in ("mem", "lat", "lon")], *refs)

    return pl.pallas_call(
        placed,
        out_shape=outs,
        in_specs=specs,
        out_specs=[VMEM_SPEC] * len(outs),
        scratch_shapes=list(scratch),
        input_output_aliases=aliases or {},
        compiler_params=pltpu.CompilerParams(vmem_limit_bytes=limit),
        cost_estimate=pl.CostEstimate(
            flops=int(us * 1e6), bytes_accessed=int(us * 3e6), transcendentals=0
        ),
    )(*args)


def in_hbm(cells):
    return pltpu.with_memory_space_constraint(cells, pltpu.HBM)


def swap(cells, axis, odd):
    count = lax.axis_size(axis)
    pairs = []
    for i in range(count):
        to = i ^ 1 if not odd else ((i + 1) ^ 1) - 1
        pairs.append((i, to % count))
    return lax.ppermute(cells, axis, pairs)


def trade(cells, axes, to):
    return lax.ppermute(cells, axes, list(enumerate(to)))


def share(cells, partner):
    return trade(cells, ("mem",), [i ^ partner for i in range(4)])


SUB = 8
TALL = 3 * ROWS
TILES = (TALL * SUB, COLS)


def put(ref, f, rows):
    ref[pl.ds(f, TALL, stride=SUB)] = rows


def pack_body(fields, first, ids, own, even, odd, *rest):
    if first:
        ext, rate, packed = rest
    else:
        terms, ext, packed, new_terms = rest
        new_terms[...] = (terms[...] + even[fields, :8]) + odd[fields, :8]
    lat = ids[1]
    is_even = lax.rem(lat, 2) == 0
    lane = lax.broadcasted_iota(jnp.int32, (TALL, COLS), 1)
    out = jnp.zeros((TALL, COLS), F32)
    for f in range(fields):
        a, b = even[f], odd[f]
        up = jnp.where(is_even, b, a)
        down = jnp.where(is_even, a, b)
        if first:
            up = jnp.where(lat == 0, 0.0, up)
            down = jnp.where(lat == 7, 0.0, down)
        whole = jnp.concatenate([up, own[f], down], axis=0)
        if f < MEMBERS:
            put(ext, f, whole)
        else:
            for sub in range(SUB):
                put(rate, sub, whole)
        at = 2 * REACH * f
        turned = pltpu.roll(whole, (at + REACH) % COLS, 1)
        out = jnp.where((lane >= at) & (lane < at + 2 * REACH), turned, out)
    packed[:TALL] = out


def pack(fields, own, even, odd, terms=()):
    return call(
        functools.partial(pack_body, fields, not terms),
        [pltpu.VMEM(TILES, F32)] * (1 if terms else 2)
        + [pltpu.VMEM((TALL + (8 if terms else 0), COLS), F32)]
        + [pltpu.VMEM((8, COLS), F32)] * len(terms),
        (own, even, odd, *terms),
        [VMEM_SPEC] * (3 + len(terms)),
        us=0.3,
    )


def ride_body(ids, held, terms, got, packed, new_terms):
    summed = terms[...] + got[...]
    new_terms[...] = summed
    packed[TALL:] = summed


def halo_of(fields, ids, even, odd):
    is_even = lax.rem(ids[2], 2) == 0
    lane = lax.broadcasted_iota(jnp.int32, (TALL, COLS), 1)
    west = lane < 0
    for f in range(fields):
        at = 2 * REACH * f
        west = west | ((lane >= at) & (lane < at + REACH))
    a, b = even[:TALL], odd[:TALL]
    return jnp.where(west, jnp.where(is_even, b, a), jnp.where(is_even, a, b))


def spread_halo(halo, f):
    return pltpu.roll(halo, (2 * COLS - REACH - 2 * REACH * f) % COLS, 1)


def sweep(adjoint, ext, side, rate):
    lane = lax.broadcasted_iota(jnp.int32, (SUB, COLS), 1)
    first, last = lane == 0, lane == COLS - 1
    low = ROWS - REACH

    def tile(row):
        return pl.ds(SUB * row, SUB)

    own = [ext[tile(low + r)] for r in range(ROWS + 2 * REACH)]
    halo = [side[tile(low + r)] for r in range(ROWS + 2 * REACH)]
    for _ in range(PASSES):
        count = len(own)
        rate_own = [rate[0, tile(low + r)] for r in range(count)]
        rate_halo = [rate[1, tile(low + r)] for r in range(count)]
        if adjoint:
            a = [v * d for v, d in zip(own, rate_own)]
            b = [v * d for v, d in zip(halo, rate_halo)]
        else:
            a, b = own, halo
        new_own, new_halo = [], []
        for r in range(1, count - 1):
            a_west, b_west = pltpu.roll(a[r], 1, 1), pltpu.roll(b[r], 1, 1)
            a_east, b_east = pltpu.roll(a[r], COLS - 1, 1), pltpu.roll(b[r], COLS - 1, 1)
            beside_a = jnp.where(first, b_west, a_west) + jnp.where(last, b_east, a_east)
            beside_b = jnp.where(first, a_west, b_west) + jnp.where(last, a_east, b_east)
            lap_a = (a[r - 1] + a[r + 1]) + beside_a - 4.0 * a[r]
            lap_b = (b[r - 1] + b[r + 1]) + beside_b - 4.0 * b[r]
            if not adjoint:
                lap_a, lap_b = rate_own[r] * lap_a, rate_halo[r] * lap_b
            new_own.append(own[r] + lap_a)
            new_halo.append(halo[r] + lap_b)
        own, halo = new_own, new_halo
        low += 1
    return own


def members_of(tiles, room):
    for r, tile in enumerate(tiles):
        room[pl.ds(SUB * r, SUB)] = tile
    return [room[pl.ds(m, ROWS, stride=SUB)] for m in range(MEMBERS)]


def partner_of(mem, partner):
    return mem + partner - 2 * (lax.rem(mem, 2) * (partner % 2)) - 4 * (lax.div(mem, 2) * (partner // 2))


def select_body(partners, own, ids, anomalies, obs_time, *rest):
    if own:
        innovation, precision, sel, inn_own, prec_own, buf, when, sems, own_sems = rest
        own = ((innovation, inn_own), (precision, prec_own))
    else:
        sel, buf, when, sems, own_sems = rest
        own = ()
    time_copy = pltpu.make_async_copy(obs_time, when, own_sems.at[2])
    time_copy.start()
    copies = []
    for g, partner in enumerate(partners):
        at = pl.ds(SHARE * partner_of(ids[0], partner), SHARE)
        for m in range(MEMBERS):
            copy = pltpu.make_async_copy(anomalies.at[m, :, at], buf.at[g, m], sems.at[g * MEMBERS + m])
            copy.start()
            copies.append(copy)
    own_copies = []
    for k, (src, dst) in enumerate(own):
        copy = pltpu.make_async_copy(src.at[pl.ds(SHARE * ids[0], SHARE)], dst, own_sems.at[k])
        copy.start()
        own_copies.append(copy)
    time_copy.wait()
    at_zero = when[...].astype(F32).astype(BF16) == 0
    for n, copy in enumerate(copies):
        g, m = divmod(n, MEMBERS)
        copy.wait()

        def plane(r, c, g=g, m=m):
            sel[g, m, r] = jnp.where(at_zero, buf[g, m, 0, r], buf[g, m, 1, r])
            return c

        lax.fori_loop(0, SHARE, plane, 0, unroll=7)
    for copy in own_copies:
        copy.wait()


def select(partners, anomalies, obs_time, own=()):
    count = len(partners)
    return call(
        functools.partial(select_body, partners, bool(own)),
        [pltpu.VMEM((count, MEMBERS, SHARE, ROWS, COLS), BF16)]
        + [pltpu.VMEM((SHARE, ROWS, COLS), F32)] * (2 if own else 0),
        (anomalies, obs_time, *own),
        [ANY_SPEC, ANY_SPEC] + ([ANY_SPEC, ANY_SPEC] if own else []),
        scratch=[
            pltpu.VMEM((count, MEMBERS, 2, SHARE, ROWS, COLS), BF16),
            pltpu.VMEM((ROWS, COLS), jnp.int32),
            pltpu.SemaphoreType.DMA((count * MEMBERS,)),
            pltpu.SemaphoreType.DMA((3,)),
        ],
        limit=16 * MIB,
        us=2.5,
    )


def share_sums(chunk, sel, w, dtype, out):
    first, count = chunk
    ws = [w[m] for m in range(MEMBERS)]

    def plane(r, c):
        total = sel[0, first + r].astype(F32) * ws[0]
        for m in range(1, MEMBERS):
            total = total + sel[m, first + r].astype(F32) * ws[m]
        out[r] = total.astype(dtype)
        return c

    lax.fori_loop(0, count, plane, 0, unroll=5 if count % 5 == 0 else 1)


def sends_body(chunk, ids, sent1, sent2, w, *outs):
    for sel, out in zip((sent1.at[0], sent1.at[1], sent2.at[0]), outs):
        share_sums(chunk, sel, w, BF16, out)


def next_sends_body(chunk, ids, sent1, sent2, w, own, *outs):
    sends_body(chunk, ids, sent1, sent2, w, *outs)


def stays_body(ids, anomalies, obs_time, w, kept, own, buf, when, sems, time_sem):
    time_copy = pltpu.make_async_copy(obs_time, when, time_sem.at[0])
    time_copy.start()
    copies = []
    for n, (first, count) in enumerate(CHUNKS):
        at = pl.ds(SHARE * ids[0] + first, count)
        for m in range(MEMBERS):
            copy = pltpu.make_async_copy(
                anomalies.at[m, :, at], buf.at[m, :, pl.ds(first, count)], sems.at[n * MEMBERS + m]
            )
            copy.start()
            copies.append(copy)
    time_copy.wait()
    at_zero = when[...].astype(F32).astype(BF16) == 0
    ws = [w[m] for m in range(MEMBERS)]
    for n, (first, count) in enumerate(CHUNKS):
        for copy in copies[n * MEMBERS : (n + 1) * MEMBERS]:
            copy.wait()

        def plane(r, c, first=first):
            total = None
            for m in range(MEMBERS):
                picked = jnp.where(at_zero, buf[m, 0, first + r], buf[m, 1, first + r])
                kept[m, first + r] = picked
                term = picked.astype(F32) * ws[m]
                total = term if total is None else total + term
            own[first + r] = total
            return c

        lax.fori_loop(0, count, plane, 0, unroll=5)


def forward_body(chunk, ids, ext, rate_own, own, even, odd, loc_norm, sent1, sent2, w, rate, terms, *rest):
    sends, side, room = rest[:-2], rest[-2], rest[-1]
    halo = halo_of(MEMBERS + 1, ids, even, odd)
    lane = lax.broadcasted_iota(jnp.int32, (TALL, COLS), 1)
    near = (lane < REACH) | (lane >= COLS - REACH)
    rate_side = jnp.where(near, spread_halo(halo, MEMBERS), 0.0)
    rate[0] = rate_own[...]
    for sub in range(SUB):
        put(rate.at[1], sub, rate_side)
    for m in range(MEMBERS):
        put(side, m, spread_halo(halo, m))
    squares = jnp.zeros((ROWS, COLS), F32)
    for m in range(MEMBERS):
        squares = squares + own[m] * own[m]
    terms[...] = squares[:8] + squares[8:]
    for m, spread in enumerate(members_of(sweep(False, ext, side, rate), room)):
        w[m] = (loc_norm[...] * spread).astype(BF16).astype(F32)
    sends_body(chunk, ids, sent1, sent2, w, *sends)


def rides(chunk):
    return 1 if chunk == CHUNKS[-1] else 0


def ridden(plane):
    plane = plane.astype(F32)
    return plane[:8] + plane[8:]


def misfit_body(chunk, factor, ids, own, got1, got2, got3, inn, prec, terms, weighted, *new_terms):
    first, count = chunk

    def plane(r, c):
        sums = (own[first + r] + got1[r].astype(F32)) + (got2[r].astype(F32) + got3[r].astype(F32))
        misfit = factor * sums - inn[first + r]
        scaled = prec[first + r] * misfit
        weighted[r] = scaled.astype(BF16)
        return c + misfit * scaled

    total = lax.fori_loop(0, count, plane, jnp.zeros((ROWS, COLS), F32), unroll=5 if count % 5 == 0 else 1)
    summed = terms[...] + (total[:8] + total[8:])
    if not rides(chunk):
        new_terms[0][...] = summed
    else:
        high = summed.astype(BF16).astype(F32)
        weighted[count] = jnp.concatenate([high, summed - high], axis=0).astype(BF16)


def pull(sel, chunk, ref, acc):
    first, count = chunk

    def plane(r, acc):
        x = ref[r].astype(F32)
        return tuple(acc[m] + sel[m, first + r].astype(F32) * x for m in range(MEMBERS))

    return lax.fori_loop(0, count, plane, acc, unroll=5 if count % 5 == 0 else 1)


def own_pull_body(ids, kept, *rest):
    refs, new = rest[:-1], rest[-1]
    acc = tuple(jnp.zeros((ROWS, COLS), F32) for _ in range(MEMBERS))
    for chunk, ref in zip(CHUNKS, refs):
        acc = pull(kept, chunk, ref, acc)
    for m in range(MEMBERS):
        new[m] = acc[m]


def pull_all(chunk, sent1, sent2, old, refs):
    acc = tuple(old[m] for m in range(MEMBERS))
    for sel, ref in zip((sent1.at[0], sent1.at[1], sent2.at[0]), refs):
        acc = pull(sel, chunk, ref, acc)
    return acc


RELAYED = 20


def pull_body(chunk, ids, sent1, sent2, old, ref1, ref2, ref3, ref4, new):
    first, count = chunk
    acc = tuple(old[m] for m in range(MEMBERS))
    acc = pull(sent1.at[0], (first, RELAYED), ref1, acc)
    acc = pull(sent1.at[0], (first + RELAYED, count - RELAYED), ref2, acc)
    acc = pull(sent1.at[1], chunk, ref3, acc)
    acc = pull(sent2.at[0], chunk, ref4, acc)
    for m in range(MEMBERS):
        new[m] = acc[m]


def last_pull_body(factor, ids, sent1, sent2, old, ref1, ref2, ref3, loc_norm, mine, new, terms):
    acc = pull_all(CHUNKS[-1], sent1, sent2, old, (ref1, ref2, ref3))
    for m in range(MEMBERS):
        new[m] = loc_norm[...] * (factor * acc[m])
    at = CHUNKS[-1][1]
    summed = (ridden(mine[at]) + ridden(ref2[at])) + (ridden(ref3[at]) + ridden(ref1[at]))
    row = lax.broadcasted_iota(jnp.int32, (8, COLS), 0)
    summed = jnp.where(row == ids[1], jnp.sum(summed, axis=0, keepdims=True), 0.0)
    terms[...] = summed
    new[MEMBERS, :8] = summed
    new[MEMBERS, 8:] = jnp.zeros((ROWS - 8, COLS), F32)


def pass_body(ids, terms, even, odd, pair, passed):
    pair[:8] = terms[...] + even[TALL:]
    pair[8:] = odd[TALL:]
    passed[...] = odd[TALL:]


def finish_body(scale, ids, held, pair, got, far_pair, far_got, out, cost):
    mine = pair[:8] + (pair[8:] + got[...])
    far = far_pair[:8] + (far_pair[8:] + far_got[...])
    cost[...] = jnp.broadcast_to(jnp.sum(mine + far) * scale, (1, COLS))
    for m in range(MEMBERS):
        out[m] = held[m]


def adjoint_body(ids, ext, even, odd, rate, control, out, side, room):
    halo = halo_of(MEMBERS, ids, even, odd)
    for m in range(MEMBERS):
        put(side, m, spread_halo(halo, m))
    for m, back in enumerate(members_of(sweep(True, ext, side, rate), room)):
        out[m] = control[m] + back


def on_device(control, anomalies, diffusivity, loc_norm, innovation, obs_precision, obs_time):
    members = MEMBERS * lax.axis_size("mem")
    cells = members * ROWS * COLS * lax.axis_size("lat") * lax.axis_size("lon")
    factor = 1.0 / math.sqrt(members - 1)
    obs_time = in_hbm(obs_time)
    anomalies = in_hbm(anomalies.reshape(MEMBERS, 2, PLANES, ROWS, COLS))
    innovation = in_hbm(innovation.reshape(PLANES, ROWS, COLS))
    obs_precision = in_hbm(obs_precision.reshape(PLANES, ROWS, COLS))
    block = (MEMBERS, ROWS, COLS)

    fields = jnp.concatenate([control, diffusivity[None]], axis=0)
    even, odd = swap(fields, "lat", False), swap(fields, "lat", True)
    sent1, inn, prec = select(PARTNERS[:2], anomalies, obs_time, (innovation, obs_precision))
    even, odd, sent1 = lax.optimization_barrier((even, odd, sent1))
    ext, rate, packed = pack(MEMBERS + 1, fields, even, odd)
    even, odd = swap(packed, "lon", False), swap(packed, "lon", True)
    (sent2,) = select(PARTNERS[2:], anomalies, obs_time)
    even, odd, sent2 = lax.optimization_barrier((even, odd, sent2))

    def blocks(count):
        return [pltpu.VMEM((count, ROWS, COLS), BF16)] * 3

    tile = pltpu.VMEM((8, COLS), F32)
    w, rate, terms, *send = call(
        functools.partial(forward_body, CHUNKS[0]),
        [pltpu.VMEM(block, F32), pltpu.VMEM((2, *TILES), F32), tile, *blocks(CHUNKS[0][1])],
        (ext, rate, fields, even, odd, loc_norm, sent1, sent2),
        [VMEM_SPEC] * 8,
        scratch=[pltpu.VMEM(TILES, F32), pltpu.VMEM((ROWS * SUB, COLS), F32)],
        us=2.0,
    )
    kept, own = call(
        stays_body,
        [pltpu.VMEM((MEMBERS, SHARE, ROWS, COLS), BF16), pltpu.VMEM((SHARE, ROWS, COLS), F32)],
        (anomalies, obs_time, w),
        [ANY_SPEC, ANY_SPEC, VMEM_SPEC],
        scratch=[
            pltpu.VMEM((MEMBERS, 2, SHARE, ROWS, COLS), BF16),
            pltpu.VMEM((ROWS, COLS), jnp.int32),
            pltpu.SemaphoreType.DMA((len(CHUNKS) * MEMBERS,)),
            pltpu.SemaphoreType.DMA((1,)),
        ],
        limit=16 * MIB,
        us=2.0,
    )
    got = []
    for i, chunk in enumerate(CHUNKS):
        if i > 0:
            send = call(
                functools.partial(next_sends_body, chunk),
                blocks(chunk[1]),
                (sent1, sent2, w, own),
                [VMEM_SPEC] * 3 + [ANY_SPEC],
                us=0.3,
            )
        got.append([share(cells, p) for cells, p in zip(send, PARTNERS)])
    weighted, near = [], []
    for i, chunk in enumerate(CHUNKS):
        piece, *rest = call(
            functools.partial(misfit_body, chunk, factor),
            [pltpu.VMEM((chunk[1] + rides(chunk), ROWS, COLS), BF16)] + [tile] * (1 - rides(chunk)),
            (own, *got[i], inn, prec, terms),
            [VMEM_SPEC] * 7,
            us=0.3,
        )
        terms = rest[0] if rest else None
        weighted.append(piece)
        if i == len(CHUNKS) - 1:
            near.append([share(piece, p) for p in PARTNERS])
        else:
            a, b = share(piece, 1), share(piece, 3)
            near.append([share(b[:RELAYED], 1), share(a[RELAYED:], 3), a, b])
    (acc,) = call(
        own_pull_body,
        [pltpu.VMEM(block, F32)],
        (kept, *weighted),
        [VMEM_SPEC] * (1 + len(CHUNKS)),
        us=0.4,
    )
    for i, chunk in enumerate(CHUNKS[:-1]):
        (acc,) = call(
            functools.partial(pull_body, chunk),
            [pltpu.VMEM(block, F32)],
            (sent1, sent2, acc, *near[i]),
            [VMEM_SPEC] * 7,
            us=0.5,
        )
    source, terms = call(
        functools.partial(last_pull_body, factor),
        [pltpu.VMEM((MEMBERS + 1, ROWS, COLS), F32), tile],
        (sent1, sent2, acc, *near[-1], loc_norm, weighted[-1]),
        [VMEM_SPEC] * 8,
        us=0.5,
    )
    even, odd = swap(source, "lat", False), swap(source, "lat", True)
    got = trade(terms, ("lat",), (2, 3, 0, 1, 6, 7, 4, 5))
    ext, packed, terms = pack(MEMBERS, source, even, odd, (terms,))
    packed, terms = call(
        ride_body,
        [pltpu.VMEM((TALL + 8, COLS), F32), tile],
        (packed, terms, got),
        [VMEM_SPEC] * 3,
        us=0.1,
        aliases={0: 0},
    )
    even, odd = swap(packed, "lon", False), swap(packed, "lon", True)
    pair, passed = call(
        pass_body, [pltpu.VMEM((16, COLS), F32), tile], (terms, even, odd), [VMEM_SPEC] * 3, us=0.1
    )
    got = swap(passed, "lon", False)
    far_pair = trade(pair, ("lat",), (4, 5, 6, 7, 0, 1, 2, 3))
    far_got = trade(passed, ("lat", "lon"), [(lat ^ 4) * 4 + (lon ^ 1) for lat in range(8) for lon in range(4)])
    even, odd, pair = lax.optimization_barrier((even, odd, pair))
    (held,) = call(
        adjoint_body,
        [pltpu.VMEM(block, F32)],
        (ext, even, odd, rate, control),
        [VMEM_SPEC] * 5,
        scratch=[pltpu.VMEM(TILES, F32), pltpu.VMEM((ROWS * SUB, COLS), F32)],
        us=3.0,
    )
    gradient, cost = call(
        functools.partial(finish_body, 0.5 / cells),
        [jax.ShapeDtypeStruct(block, F32), jax.ShapeDtypeStruct((1, COLS), F32)],
        (held, pair, got, far_pair, far_got),
        [VMEM_SPEC] * 5,
        us=0.1,
    )
    return gradient, cost[0, 0]


def solution(mesh):
    return jax.shard_map(
        on_device,
        mesh=mesh,
        in_specs=(
            P("mem", "lat", "lon"),
            P("mem", None, None, None, "lat", "lon"),
            P("lat", "lon"),
            P("lat", "lon"),
            P(None, None, "lat", "lon"),
            P(None, None, "lat", "lon"),
            P("lat", "lon"),
        ),
        out_specs=(P("mem", "lat", "lon"), P()),
        check_vma=False,
    )
```

```python
import functools
import math

import jax
import jax.numpy as jnp
from jax import lax
from jax.experimental import pallas as pl
from jax.experimental.pallas import tpu as pltpu
from jax.sharding import PartitionSpec as P

F32 = jnp.float32
BF16 = jnp.bfloat16
PASSES = 10
REACH = 10
ROWS, COLS = 16, 128
MEMBERS = 5
PLANES = 280
SHARE = PLANES // 4
CHUNKS = ((0, 40), (40, 30))
PARTNERS = (2, 1, 3)
MIB = 1 << 20

VMEM_SPEC = pl.BlockSpec(memory_space=pltpu.VMEM)
ANY_SPEC = pl.BlockSpec(memory_space=pl.ANY)


def call(body, outs, args, specs, scratch=(), limit=8 * MIB, us=1.0, aliases=None):
    def placed(*refs):
        body([lax.axis_index(a) for a in ("mem", "lat", "lon")], *refs)

    return pl.pallas_call(
        placed,
        out_shape=outs,
        in_specs=specs,
        out_specs=[VMEM_SPEC] * len(outs),
        scratch_shapes=list(scratch),
        input_output_aliases=aliases or {},
        compiler_params=pltpu.CompilerParams(vmem_limit_bytes=limit),
        cost_estimate=pl.CostEstimate(
            flops=int(us * 1e6), bytes_accessed=int(us * 3e6), transcendentals=0
        ),
    )(*args)


def in_hbm(cells):
    return pltpu.with_memory_space_constraint(cells, pltpu.HBM)


def swap(cells, axis, odd):
    count = lax.axis_size(axis)
    pairs = []
    for i in range(count):
        to = i ^ 1 if not odd else ((i + 1) ^ 1) - 1
        pairs.append((i, to % count))
    return lax.ppermute(cells, axis, pairs)


def trade(cells, axes, to):
    return lax.ppermute(cells, axes, list(enumerate(to)))


def share(cells, partner):
    return trade(cells, ("mem",), [i ^ partner for i in range(4)])


SUB = 8
TALL = 3 * ROWS
TILES = (TALL * SUB, COLS)


def put(ref, f, rows):
    ref[pl.ds(f, TALL, stride=SUB)] = rows


def split(terms):
    high = terms.astype(BF16).astype(F32)
    return jnp.concatenate([high, terms - high], axis=0).astype(BF16)


def ridden(plane):
    plane = plane.astype(F32)
    return plane[:8] + plane[8:]


def join_body(ids, control, diffusivity, out, room, sems):
    copies = (
        pltpu.make_async_copy(control, room.at[pl.ds(0, MEMBERS)], sems.at[0]),
        pltpu.make_async_copy(diffusivity, room.at[MEMBERS], sems.at[1]),
    )
    for copy in copies:
        copy.start()
    for copy in copies:
        copy.wait()
    out[...] = room[...].astype(BF16)


def pack_body(fields, ids, *refs):
    if fields > MEMBERS:
        control, diffusivity, even, odd, ext, rate, packed = refs
        own = [control[m] for m in range(MEMBERS)] + [diffusivity[...]]
    else:
        source, terms, even, odd, ext, packed, new_terms = refs
        own = [source[m] for m in range(MEMBERS)]
        new_terms[...] = (terms[...] + ridden(even[fields])) + ridden(odd[fields])
    lat = ids[1]
    is_even = lax.rem(lat, 2) == 0
    lane = lax.broadcasted_iota(jnp.int32, (TALL, COLS), 1)
    out = jnp.zeros((TALL, COLS), F32)
    for f in range(fields):
        a, b = even[f].astype(F32), odd[f].astype(F32)
        up = jnp.where(is_even, b, a)
        down = jnp.where(is_even, a, b)
        if fields > MEMBERS:
            up = jnp.where(lat == 0, 0.0, up)
            down = jnp.where(lat == 7, 0.0, down)
        whole = jnp.concatenate([up, own[f], down], axis=0)
        if f < MEMBERS:
            put(ext, f, whole)
        else:
            for sub in range(SUB):
                put(rate, sub, whole)
        at = 2 * REACH * f
        turned = pltpu.roll(whole, (at + REACH) % COLS, 1)
        out = jnp.where((lane >= at) & (lane < at + 2 * REACH), turned, out)
    packed[:TALL] = out.astype(BF16)


def pack(fields, own, even, odd):
    first = fields > MEMBERS
    return call(
        functools.partial(pack_body, fields),
        [pltpu.VMEM(TILES, F32)] * (2 if first else 1)
        + [pltpu.VMEM((TALL + (0 if first else 16), COLS), BF16)]
        + [pltpu.VMEM((8, COLS), F32)] * (0 if first else 1),
        (*own, even, odd),
        [VMEM_SPEC] * 4,
        us=0.3,
    )


def ride_body(ids, held, terms, got, packed, new_terms):
    plane = split(terms[...] + got[...])
    new_terms[...] = ridden(plane)
    packed[TALL:] = plane


def halo_of(fields, ids, even, odd):
    is_even = lax.rem(ids[2], 2) == 0
    lane = lax.broadcasted_iota(jnp.int32, (TALL, COLS), 1)
    west = lane < 0
    for f in range(fields):
        at = 2 * REACH * f
        west = west | ((lane >= at) & (lane < at + REACH))
    a, b = even[:TALL].astype(F32), odd[:TALL].astype(F32)
    return jnp.where(west, jnp.where(is_even, b, a), jnp.where(is_even, a, b))


def spread_halo(halo, f):
    return pltpu.roll(halo, (2 * COLS - REACH - 2 * REACH * f) % COLS, 1)


def sweep(adjoint, ext, side, rate):
    lane = lax.broadcasted_iota(jnp.int32, (SUB, COLS), 1)
    first, last = lane == 0, lane == COLS - 1
    low = ROWS - REACH

    def tile(row):
        return pl.ds(SUB * row, SUB)

    own = [ext[tile(low + r)] for r in range(ROWS + 2 * REACH)]
    halo = [side[tile(low + r)] for r in range(ROWS + 2 * REACH)]
    for _ in range(PASSES):
        count = len(own)
        rate_own = [rate[0, tile(low + r)] for r in range(count)]
        rate_halo = [rate[1, tile(low + r)] for r in range(count)]
        if adjoint:
            a = [v * d for v, d in zip(own, rate_own)]
            b = [v * d for v, d in zip(halo, rate_halo)]
        else:
            a, b = own, halo
        new_own, new_halo = [], []
        for r in range(1, count - 1):
            a_west, b_west = pltpu.roll(a[r], 1, 1), pltpu.roll(b[r], 1, 1)
            a_east, b_east = pltpu.roll(a[r], COLS - 1, 1), pltpu.roll(b[r], COLS - 1, 1)
            beside_a = jnp.where(first, b_west, a_west) + jnp.where(last, b_east, a_east)
            beside_b = jnp.where(first, a_west, b_west) + jnp.where(last, a_east, b_east)
            lap_a = (a[r - 1] + a[r + 1]) + beside_a - 4.0 * a[r]
            lap_b = (b[r - 1] + b[r + 1]) + beside_b - 4.0 * b[r]
            if not adjoint:
                lap_a, lap_b = rate_own[r] * lap_a, rate_halo[r] * lap_b
            new_own.append(own[r] + lap_a)
            new_halo.append(halo[r] + lap_b)
        own, halo = new_own, new_halo
        low += 1
    return own


def members_of(tiles, room):
    for r, tile in enumerate(tiles):
        room[pl.ds(SUB * r, SUB)] = tile
    return [room[pl.ds(m, ROWS, stride=SUB)] for m in range(MEMBERS)]


def partner_of(mem, partner):
    return mem + partner - 2 * (lax.rem(mem, 2) * (partner % 2)) - 4 * (lax.div(mem, 2) * (partner // 2))


def select_body(partners, own, ids, anomalies, obs_time, *rest):
    if own:
        innovation, precision, sel, inn_own, prec_own, buf, when, sems, own_sems = rest
        own = ((innovation, inn_own), (precision, prec_own))
    else:
        sel, buf, when, sems, own_sems = rest
        own = ()
    time_copy = pltpu.make_async_copy(obs_time, when, own_sems.at[2])
    time_copy.start()
    copies = []
    for g, partner in enumerate(partners):
        at = pl.ds(SHARE * partner_of(ids[0], partner), SHARE)
        for m in range(MEMBERS):
            copy = pltpu.make_async_copy(anomalies.at[m, :, at], buf.at[g, m], sems.at[g * MEMBERS + m])
            copy.start()
            copies.append(copy)
    own_copies = []
    for k, (src, dst) in enumerate(own):
        copy = pltpu.make_async_copy(src.at[pl.ds(SHARE * ids[0], SHARE)], dst, own_sems.at[k])
        copy.start()
        own_copies.append(copy)
    time_copy.wait()
    at_zero = when[...].astype(F32).astype(BF16) == 0
    for n, copy in enumerate(copies):
        g, m = divmod(n, MEMBERS)
        copy.wait()

        def plane(r, c, g=g, m=m):
            sel[g, m, r] = jnp.where(at_zero, buf[g, m, 0, r], buf[g, m, 1, r])
            return c

        lax.fori_loop(0, SHARE, plane, 0, unroll=7)
    for copy in own_copies:
        copy.wait()


def select(partners, anomalies, obs_time, own=()):
    count = len(partners)
    return call(
        functools.partial(select_body, partners, bool(own)),
        [pltpu.VMEM((count, MEMBERS, SHARE, ROWS, COLS), BF16)]
        + [pltpu.VMEM((SHARE, ROWS, COLS), F32)] * (2 if own else 0),
        (anomalies, obs_time, *own),
        [ANY_SPEC, ANY_SPEC] + ([ANY_SPEC, ANY_SPEC] if own else []),
        scratch=[
            pltpu.VMEM((count, MEMBERS, 2, SHARE, ROWS, COLS), BF16),
            pltpu.VMEM((ROWS, COLS), jnp.int32),
            pltpu.SemaphoreType.DMA((count * MEMBERS,)),
            pltpu.SemaphoreType.DMA((3,)),
        ],
        limit=16 * MIB,
        us=2.5,
    )


def share_sums(chunk, sel, w, dtype, out):
    first, count = chunk
    ws = [w[m] for m in range(MEMBERS)]

    def plane(r, c):
        total = sel[0, first + r].astype(F32) * ws[0]
        for m in range(1, MEMBERS):
            total = total + sel[m, first + r].astype(F32) * ws[m]
        out[r] = total.astype(dtype)
        return c

    lax.fori_loop(0, count, plane, 0, unroll=5 if count % 5 == 0 else 1)


def sends_body(chunk, ids, sent1, sent2, w, *outs):
    for sel, out in zip((sent1.at[0], sent1.at[1], sent2.at[0]), outs):
        share_sums(chunk, sel, w, BF16, out)


def next_sends_body(chunk, ids, sent1, sent2, w, own, *outs):
    sends_body(chunk, ids, sent1, sent2, w, *outs)


def stays_body(ids, anomalies, obs_time, w, kept, own, buf, when, sems, time_sem):
    time_copy = pltpu.make_async_copy(obs_time, when, time_sem.at[0])
    time_copy.start()
    copies = []
    for n, (first, count) in enumerate(CHUNKS):
        at = pl.ds(SHARE * ids[0] + first, count)
        for m in range(MEMBERS):
            copy = pltpu.make_async_copy(
                anomalies.at[m, :, at], buf.at[m, :, pl.ds(first, count)], sems.at[n * MEMBERS + m]
            )
            copy.start()
            copies.append(copy)
    time_copy.wait()
    at_zero = when[...].astype(F32).astype(BF16) == 0
    ws = [w[m] for m in range(MEMBERS)]
    for n, (first, count) in enumerate(CHUNKS):
        for copy in copies[n * MEMBERS : (n + 1) * MEMBERS]:
            copy.wait()

        def plane(r, c, first=first):
            total = None
            for m in range(MEMBERS):
                picked = jnp.where(at_zero, buf[m, 0, first + r], buf[m, 1, first + r])
                kept[m, first + r] = picked
                term = picked.astype(F32) * ws[m]
                total = term if total is None else total + term
            own[first + r] = total
            return c

        lax.fori_loop(0, count, plane, 0, unroll=5)


def forward_body(chunk, ids, ext, rate_own, control, even, odd, loc_norm, sent1, sent2, w, rate, terms, *rest):
    sends, side, room = rest[:-2], rest[-2], rest[-1]
    halo = halo_of(MEMBERS + 1, ids, even, odd)
    lane = lax.broadcasted_iota(jnp.int32, (TALL, COLS), 1)
    near = (lane < REACH) | (lane >= COLS - REACH)
    rate_side = jnp.where(near, spread_halo(halo, MEMBERS), 0.0)
    rate[0] = rate_own[...]
    for sub in range(SUB):
        put(rate.at[1], sub, rate_side)
    for m in range(MEMBERS):
        put(side, m, spread_halo(halo, m))
    squares = jnp.zeros((ROWS, COLS), F32)
    for m in range(MEMBERS):
        squares = squares + control[m] * control[m]
    terms[...] = squares[:8] + squares[8:]
    for m, spread in enumerate(members_of(sweep(False, ext, side, rate), room)):
        w[m] = (loc_norm[...] * spread).astype(BF16).astype(F32)
    sends_body(chunk, ids, sent1, sent2, w, *sends)


def rides(chunk):
    return 1 if chunk == CHUNKS[-1] else 0


def misfit_body(chunk, factor, ids, own, got1, got2, got3, inn, prec, terms, weighted, *new_terms):
    first, count = chunk

    def plane(r, c):
        sums = (own[first + r] + got1[r].astype(F32)) + (got2[r].astype(F32) + got3[r].astype(F32))
        misfit = factor * sums - inn[first + r]
        scaled = prec[first + r] * misfit
        weighted[r] = scaled.astype(BF16)
        return c + misfit * scaled

    total = lax.fori_loop(0, count, plane, jnp.zeros((ROWS, COLS), F32), unroll=5 if count % 5 == 0 else 1)
    summed = terms[...] + (total[:8] + total[8:])
    if not rides(chunk):
        new_terms[0][...] = summed
    else:
        weighted[count] = split(summed)


def pull(sel, chunk, ref, acc):
    first, count = chunk

    def plane(r, acc):
        x = ref[r].astype(F32)
        return tuple(acc[m] + sel[m, first + r].astype(F32) * x for m in range(MEMBERS))

    return lax.fori_loop(0, count, plane, acc, unroll=5 if count % 5 == 0 else 1)


def own_pull_body(ids, kept, *rest):
    refs, new = rest[:-1], rest[-1]
    acc = tuple(jnp.zeros((ROWS, COLS), F32) for _ in range(MEMBERS))
    for chunk, ref in zip(CHUNKS, refs):
        acc = pull(kept, chunk, ref, acc)
    for m in range(MEMBERS):
        new[m] = acc[m]


def pull_all(chunk, sent1, sent2, old, refs):
    acc = tuple(old[m] for m in range(MEMBERS))
    for sel, ref in zip((sent1.at[0], sent1.at[1], sent2.at[0]), refs):
        acc = pull(sel, chunk, ref, acc)
    return acc


RELAYED = 20


def pull_body(chunk, ids, sent1, sent2, old, ref1, ref2, ref3, ref4, new):
    first, count = chunk
    acc = tuple(old[m] for m in range(MEMBERS))
    acc = pull(sent1.at[0], (first, RELAYED), ref1, acc)
    acc = pull(sent1.at[0], (first + RELAYED, count - RELAYED), ref2, acc)
    acc = pull(sent1.at[1], chunk, ref3, acc)
    acc = pull(sent2.at[0], chunk, ref4, acc)
    for m in range(MEMBERS):
        new[m] = acc[m]


def last_pull_body(factor, ids, sent1, sent2, old, ref1, ref2, ref3, loc_norm, mine, new, halo, terms):
    acc = pull_all(CHUNKS[-1], sent1, sent2, old, (ref1, ref2, ref3))
    for m in range(MEMBERS):
        source = loc_norm[...] * (factor * acc[m])
        new[m] = source
        halo[m] = source.astype(BF16)
    at = CHUNKS[-1][1]
    summed = (ridden(mine[at]) + ridden(ref2[at])) + (ridden(ref3[at]) + ridden(ref1[at]))
    row = lax.broadcasted_iota(jnp.int32, (8, COLS), 0)
    plane = split(jnp.where(row == ids[1], jnp.sum(summed, axis=0, keepdims=True), 0.0))
    halo[MEMBERS] = plane
    terms[...] = ridden(plane)


def pass_body(ids, terms, even, odd, pair, passed):
    other = ridden(odd[TALL:])
    pair[:8] = terms[...] + ridden(even[TALL:])
    pair[8:] = other
    passed[...] = other


def finish_body(scale, ids, held, pair, got, far_pair, far_got, out, cost):
    mine = pair[:8] + (pair[8:] + got[...])
    far = far_pair[:8] + (far_pair[8:] + far_got[...])
    cost[...] = jnp.broadcast_to(jnp.sum(mine + far) * scale, (1, COLS))
    for m in range(MEMBERS):
        out[m] = held[m]


def adjoint_body(ids, ext, even, odd, rate, control, out, side, room):
    halo = halo_of(MEMBERS, ids, even, odd)
    for m in range(MEMBERS):
        put(side, m, spread_halo(halo, m))
    for m, back in enumerate(members_of(sweep(True, ext, side, rate), room)):
        out[m] = control[m] + back


def on_device(control, anomalies, diffusivity, loc_norm, innovation, obs_precision, obs_time):
    members = MEMBERS * lax.axis_size("mem")
    cells = members * ROWS * COLS * lax.axis_size("lat") * lax.axis_size("lon")
    factor = 1.0 / math.sqrt(members - 1)
    obs_time = in_hbm(obs_time)
    anomalies = in_hbm(anomalies.reshape(MEMBERS, 2, PLANES, ROWS, COLS))
    innovation = in_hbm(innovation.reshape(PLANES, ROWS, COLS))
    obs_precision = in_hbm(obs_precision.reshape(PLANES, ROWS, COLS))
    block = (MEMBERS, ROWS, COLS)

    (fields,) = call(
        join_body,
        [pltpu.VMEM((MEMBERS + 1, ROWS, COLS), BF16)],
        (in_hbm(control), in_hbm(diffusivity)),
        [ANY_SPEC] * 2,
        scratch=[pltpu.VMEM((MEMBERS + 1, ROWS, COLS), F32), pltpu.SemaphoreType.DMA((2,))],
        us=0.5,
    )
    even, odd = swap(fields, "lat", False), swap(fields, "lat", True)
    sent1, inn, prec = select(PARTNERS[:2], anomalies, obs_time, (innovation, obs_precision))
    even, odd, sent1 = lax.optimization_barrier((even, odd, sent1))
    ext, rate, packed = pack(MEMBERS + 1, (control, diffusivity), even, odd)
    even, odd = swap(packed, "lon", False), swap(packed, "lon", True)
    (sent2,) = select(PARTNERS[2:], anomalies, obs_time)
    even, odd, sent2 = lax.optimization_barrier((even, odd, sent2))

    def blocks(count):
        return [pltpu.VMEM((count, ROWS, COLS), BF16)] * 3

    tile = pltpu.VMEM((8, COLS), F32)
    w, rate, terms, *send = call(
        functools.partial(forward_body, CHUNKS[0]),
        [pltpu.VMEM(block, F32), pltpu.VMEM((2, *TILES), F32), tile, *blocks(CHUNKS[0][1])],
        (ext, rate, control, even, odd, loc_norm, sent1, sent2),
        [VMEM_SPEC] * 8,
        scratch=[pltpu.VMEM(TILES, F32), pltpu.VMEM((ROWS * SUB, COLS), F32)],
        us=2.0,
    )
    kept, own = call(
        stays_body,
        [pltpu.VMEM((MEMBERS, SHARE, ROWS, COLS), BF16), pltpu.VMEM((SHARE, ROWS, COLS), F32)],
        (anomalies, obs_time, w),
        [ANY_SPEC, ANY_SPEC, VMEM_SPEC],
        scratch=[
            pltpu.VMEM((MEMBERS, 2, SHARE, ROWS, COLS), BF16),
            pltpu.VMEM((ROWS, COLS), jnp.int32),
            pltpu.SemaphoreType.DMA((len(CHUNKS) * MEMBERS,)),
            pltpu.SemaphoreType.DMA((1,)),
        ],
        limit=16 * MIB,
        us=2.0,
    )
    got = []
    for i, chunk in enumerate(CHUNKS):
        if i > 0:
            send = call(
                functools.partial(next_sends_body, chunk),
                blocks(chunk[1]),
                (sent1, sent2, w, own),
                [VMEM_SPEC] * 3 + [ANY_SPEC],
                us=0.3,
            )
        got.append([share(cells, p) for cells, p in zip(send, PARTNERS)])
    weighted, near = [], []
    for i, chunk in enumerate(CHUNKS):
        piece, *rest = call(
            functools.partial(misfit_body, chunk, factor),
            [pltpu.VMEM((chunk[1] + rides(chunk), ROWS, COLS), BF16)] + [tile] * (1 - rides(chunk)),
            (own, *got[i], inn, prec, terms),
            [VMEM_SPEC] * 7,
            us=0.3,
        )
        terms = rest[0] if rest else None
        weighted.append(piece)
        if i == len(CHUNKS) - 1:
            near.append([share(piece, p) for p in PARTNERS])
        else:
            a, b = share(piece, 1), share(piece, 3)
            near.append([share(b[:RELAYED], 1), share(a[RELAYED:], 3), a, b])
    (acc,) = call(
        own_pull_body,
        [pltpu.VMEM(block, F32)],
        (kept, *weighted),
        [VMEM_SPEC] * (1 + len(CHUNKS)),
        us=0.4,
    )
    for i, chunk in enumerate(CHUNKS[:-1]):
        (acc,) = call(
            functools.partial(pull_body, chunk),
            [pltpu.VMEM(block, F32)],
            (sent1, sent2, acc, *near[i]),
            [VMEM_SPEC] * 7,
            us=0.5,
        )
    source, halo, terms = call(
        functools.partial(last_pull_body, factor),
        [
            pltpu.VMEM(block, F32),
            pltpu.VMEM((MEMBERS + 1, ROWS, COLS), BF16),
            tile,
        ],
        (sent1, sent2, acc, *near[-1], loc_norm, weighted[-1]),
        [VMEM_SPEC] * 8,
        us=0.5,
    )
    got = trade(terms, ("lat",), (2, 3, 0, 1, 6, 7, 4, 5))
    even, odd = swap(halo, "lat", False), swap(halo, "lat", True)
    ext, packed, terms = pack(MEMBERS, (source, terms), even, odd)
    packed, terms = call(
        ride_body,
        [pltpu.VMEM((TALL + 16, COLS), BF16), tile],
        (packed, terms, got),
        [VMEM_SPEC] * 3,
        us=0.1,
        aliases={0: 0},
    )
    even, odd = swap(packed, "lon", False), swap(packed, "lon", True)
    pair, passed = call(
        pass_body, [pltpu.VMEM((16, COLS), F32), tile], (terms, even, odd), [VMEM_SPEC] * 3, us=0.1
    )
    got = swap(passed, "lon", False)
    far_pair = trade(pair, ("lat",), (4, 5, 6, 7, 0, 1, 2, 3))
    far_got = trade(passed, ("lat", "lon"), [(lat ^ 4) * 4 + (lon ^ 1) for lat in range(8) for lon in range(4)])
    even, odd, pair = lax.optimization_barrier((even, odd, pair))
    (held,) = call(
        adjoint_body,
        [pltpu.VMEM(block, F32)],
        (ext, even, odd, rate, control),
        [VMEM_SPEC] * 5,
        scratch=[pltpu.VMEM(TILES, F32), pltpu.VMEM((ROWS * SUB, COLS), F32)],
        us=3.0,
    )
    gradient, cost = call(
        functools.partial(finish_body, 0.5 / cells),
        [jax.ShapeDtypeStruct(block, F32), jax.ShapeDtypeStruct((1, COLS), F32)],
        (held, pair, got, far_pair, far_got),
        [VMEM_SPEC] * 5,
        us=0.1,
    )
    return gradient, cost[0, 0]


def solution(mesh):
    return jax.shard_map(
        on_device,
        mesh=mesh,
        in_specs=(
            P("mem", "lat", "lon"),
            P("mem", None, None, None, "lat", "lon"),
            P("lat", "lon"),
            P("lat", "lon"),
            P(None, None, "lat", "lon"),
            P(None, None, "lat", "lon"),
            P("lat", "lon"),
        ),
        out_specs=(P("mem", "lat", "lon"), P()),
        check_vma=False,
    )
```

```python
import functools
import math

import jax
import jax.numpy as jnp
from jax import lax
from jax.experimental import pallas as pl
from jax.experimental.pallas import tpu as pltpu
from jax.sharding import PartitionSpec as P

F32 = jnp.float32
BF16 = jnp.bfloat16
PASSES = 10
REACH = 10
ROWS, COLS = 16, 128
MEMBERS = 5
PLANES = 280
SHARE = PLANES // 4
CHUNKS = ((0, 40), (40, 30))
PARTNERS = (2, 1, 3)
MIB = 1 << 20

VMEM_SPEC = pl.BlockSpec(memory_space=pltpu.VMEM)
ANY_SPEC = pl.BlockSpec(memory_space=pl.ANY)


def call(body, outs, args, specs, scratch=(), limit=8 * MIB, us=1.0, aliases=None):
    def placed(*refs):
        body([lax.axis_index(a) for a in ("mem", "lat", "lon")], *refs)

    return pl.pallas_call(
        placed,
        out_shape=outs,
        in_specs=specs,
        out_specs=[VMEM_SPEC] * len(outs),
        scratch_shapes=list(scratch),
        input_output_aliases=aliases or {},
        compiler_params=pltpu.CompilerParams(vmem_limit_bytes=limit),
        cost_estimate=pl.CostEstimate(
            flops=int(us * 1e6), bytes_accessed=int(us * 3e6), transcendentals=0
        ),
    )(*args)


def in_hbm(cells):
    return pltpu.with_memory_space_constraint(cells, pltpu.HBM)


def swap(cells, axis, odd):
    count = lax.axis_size(axis)
    pairs = []
    for i in range(count):
        to = i ^ 1 if not odd else ((i + 1) ^ 1) - 1
        pairs.append((i, to % count))
    return lax.ppermute(cells, axis, pairs)


def trade(cells, axes, to):
    return lax.ppermute(cells, axes, list(enumerate(to)))


def share(cells, partner):
    return trade(cells, ("mem",), [i ^ partner for i in range(4)])


SUB = 8
TALL = 3 * ROWS
TILES = (TALL * SUB, COLS)


def put(ref, f, rows):
    ref[pl.ds(f, TALL, stride=SUB)] = rows


def split(terms):
    high = terms.astype(BF16).astype(F32)
    return jnp.concatenate([high, terms - high], axis=0).astype(BF16)


def ridden(plane):
    plane = plane.astype(F32)
    return plane[:8] + plane[8:]


def join_body(ids, control, diffusivity, out, room, sems):
    copies = (
        pltpu.make_async_copy(control, room.at[pl.ds(0, MEMBERS)], sems.at[0]),
        pltpu.make_async_copy(diffusivity, room.at[MEMBERS], sems.at[1]),
    )
    for copy in copies:
        copy.start()
    for copy in copies:
        copy.wait()
    out[...] = room[...].astype(BF16)


def pack_body(fields, ids, *refs):
    if fields > MEMBERS:
        control, diffusivity, even, odd, ext, rate, packed = refs
        own = [control[m] for m in range(MEMBERS)] + [diffusivity[...]]
    else:
        source, terms, even, odd, ext, packed, new_terms = refs
        own = [source[m] for m in range(MEMBERS)]
        new_terms[...] = (terms[...] + ridden(even[fields])) + ridden(odd[fields])
    lat = ids[1]
    is_even = lax.rem(lat, 2) == 0
    lane = lax.broadcasted_iota(jnp.int32, (TALL, COLS), 1)
    out = jnp.zeros((TALL, COLS), F32)
    for f in range(fields):
        a, b = even[f].astype(F32), odd[f].astype(F32)
        up = jnp.where(is_even, b, a)
        down = jnp.where(is_even, a, b)
        if fields > MEMBERS:
            up = jnp.where(lat == 0, 0.0, up)
            down = jnp.where(lat == 7, 0.0, down)
        whole = jnp.concatenate([up, own[f], down], axis=0)
        if f < MEMBERS:
            put(ext, f, whole)
        else:
            for sub in range(SUB):
                put(rate, sub, whole)
        at = 2 * REACH * f
        turned = pltpu.roll(whole, (at + REACH) % COLS, 1)
        out = jnp.where((lane >= at) & (lane < at + 2 * REACH), turned, out)
    packed[:TALL] = out.astype(BF16)


def pack(fields, own, even, odd):
    first = fields > MEMBERS
    return call(
        functools.partial(pack_body, fields),
        [pltpu.VMEM(TILES, F32)] * (2 if first else 1)
        + [pltpu.VMEM((TALL + (0 if first else 16), COLS), BF16)]
        + [pltpu.VMEM((8, COLS), F32)] * (0 if first else 1),
        (*own, even, odd),
        [VMEM_SPEC] * 4,
        us=0.3,
    )


def ride_body(ids, held, terms, got, packed, new_terms):
    plane = split(terms[...] + got[...])
    new_terms[...] = ridden(plane)
    packed[TALL:] = plane


def halo_of(fields, ids, even, odd):
    is_even = lax.rem(ids[2], 2) == 0
    lane = lax.broadcasted_iota(jnp.int32, (TALL, COLS), 1)
    west = lane < 0
    for f in range(fields):
        at = 2 * REACH * f
        west = west | ((lane >= at) & (lane < at + REACH))
    a, b = even[:TALL].astype(F32), odd[:TALL].astype(F32)
    return jnp.where(west, jnp.where(is_even, b, a), jnp.where(is_even, a, b))


def spread_halo(halo, f):
    return pltpu.roll(halo, (2 * COLS - REACH - 2 * REACH * f) % COLS, 1)


def sweep(adjoint, ext, side, rate):
    lane = lax.broadcasted_iota(jnp.int32, (SUB, COLS), 1)
    first, last = lane == 0, lane == COLS - 1
    low = ROWS - REACH

    def tile(row):
        return pl.ds(SUB * row, SUB)

    own = [ext[tile(low + r)] for r in range(ROWS + 2 * REACH)]
    halo = [side[tile(low + r)] for r in range(ROWS + 2 * REACH)]
    for _ in range(PASSES):
        count = len(own)
        rate_own = [rate[0, tile(low + r)] for r in range(count)]
        rate_halo = [rate[1, tile(low + r)] for r in range(count)]
        if adjoint:
            a = [v * d for v, d in zip(own, rate_own)]
            b = [v * d for v, d in zip(halo, rate_halo)]
        else:
            a, b = own, halo
        new_own, new_halo = [], []
        for r in range(1, count - 1):
            a_west, b_west = pltpu.roll(a[r], 1, 1), pltpu.roll(b[r], 1, 1)
            a_east, b_east = pltpu.roll(a[r], COLS - 1, 1), pltpu.roll(b[r], COLS - 1, 1)
            beside_a = jnp.where(first, b_west, a_west) + jnp.where(last, b_east, a_east)
            beside_b = jnp.where(first, a_west, b_west) + jnp.where(last, a_east, b_east)
            lap_a = (a[r - 1] + a[r + 1]) + beside_a - 4.0 * a[r]
            lap_b = (b[r - 1] + b[r + 1]) + beside_b - 4.0 * b[r]
            if not adjoint:
                lap_a, lap_b = rate_own[r] * lap_a, rate_halo[r] * lap_b
            new_own.append(own[r] + lap_a)
            new_halo.append(halo[r] + lap_b)
        own, halo = new_own, new_halo
        low += 1
    return own


def members_of(tiles, room):
    for r, tile in enumerate(tiles):
        room[pl.ds(SUB * r, SUB)] = tile
    return [room[pl.ds(m, ROWS, stride=SUB)] for m in range(MEMBERS)]


def partner_of(mem, partner):
    return mem + partner - 2 * (lax.rem(mem, 2) * (partner % 2)) - 4 * (lax.div(mem, 2) * (partner // 2))


def select_body(partners, planes, own, ids, anomalies, obs_time, *rest):
    if own:
        innovation, precision, sel, inn_own, prec_own, buf, when, sems, own_sems = rest
        own = ((innovation, inn_own), (precision, prec_own))
    else:
        sel, buf, when, sems, own_sems = rest
        own = ()
    time_copy = pltpu.make_async_copy(obs_time, when, own_sems.at[2])
    time_copy.start()
    copies = []
    for g, partner in enumerate(partners):
        at = pl.ds(SHARE * partner_of(ids[0], partner), planes)
        for m in range(MEMBERS):
            copy = pltpu.make_async_copy(anomalies.at[m, :, at], buf.at[g, m], sems.at[g * MEMBERS + m])
            copy.start()
            copies.append(copy)
    own_copies = []
    for k, (src, dst) in enumerate(own):
        copy = pltpu.make_async_copy(src.at[pl.ds(SHARE * ids[0], SHARE)], dst, own_sems.at[k])
        copy.start()
        own_copies.append(copy)
    time_copy.wait()
    at_zero = when[...].astype(F32).astype(BF16) == 0
    for n, copy in enumerate(copies):
        g, m = divmod(n, MEMBERS)
        copy.wait()

        def plane(r, c, g=g, m=m):
            sel[g, m, r] = jnp.where(at_zero, buf[g, m, 0, r], buf[g, m, 1, r])
            return c

        lax.fori_loop(0, planes, plane, 0, unroll=5)
    for copy in own_copies:
        copy.wait()


def select(partners, planes, anomalies, obs_time, own=()):
    count = len(partners)
    return call(
        functools.partial(select_body, partners, planes, bool(own)),
        [pltpu.VMEM((count, MEMBERS, planes, ROWS, COLS), BF16)]
        + [pltpu.VMEM((SHARE, ROWS, COLS), F32)] * (2 if own else 0),
        (anomalies, obs_time, *own),
        [ANY_SPEC, ANY_SPEC] + ([ANY_SPEC, ANY_SPEC] if own else []),
        scratch=[
            pltpu.VMEM((count, MEMBERS, 2, planes, ROWS, COLS), BF16),
            pltpu.VMEM((ROWS, COLS), jnp.int32),
            pltpu.SemaphoreType.DMA((count * MEMBERS,)),
            pltpu.SemaphoreType.DMA((3,)),
        ],
        limit=16 * MIB,
        us=2.5,
    )


def share_sums(chunk, sel, w, dtype, out):
    first, count = chunk
    ws = [w[m] for m in range(MEMBERS)]

    def plane(r, c):
        total = sel[0, first + r].astype(F32) * ws[0]
        for m in range(1, MEMBERS):
            total = total + sel[m, first + r].astype(F32) * ws[m]
        out[r] = total.astype(dtype)
        return c

    lax.fori_loop(0, count, plane, 0, unroll=5 if count % 5 == 0 else 1)


def sends_body(chunk, ids, sent1, sent2, w, *outs):
    for sel, out in zip((sent1.at[0], sent1.at[1], sent2.at[0]), outs):
        share_sums(chunk, sel, w, BF16, out)


def next_sends_body(chunk, ids, sent1, later, w, own, out1, out2, out3):
    share_sums(chunk, sent1.at[0], w, BF16, out1)
    share_sums(chunk, sent1.at[1], w, BF16, out2)
    share_sums((0, chunk[1]), later, w, BF16, out3)


def stays_body(ids, anomalies, obs_time, w, kept, own, later, buf, rest, when, sems, time_sem):
    time_copy = pltpu.make_async_copy(obs_time, when, time_sem.at[0])
    time_copy.start()
    copies = []
    for n, (first, count) in enumerate(CHUNKS):
        at = pl.ds(SHARE * ids[0] + first, count)
        for m in range(MEMBERS):
            copy = pltpu.make_async_copy(
                anomalies.at[m, :, at], buf.at[m, :, pl.ds(first, count)], sems.at[n * MEMBERS + m]
            )
            copy.start()
            copies.append(copy)
    first, count = CHUNKS[1]
    at = pl.ds(SHARE * partner_of(ids[0], PARTNERS[2]) + first, count)
    rest_copies = []
    for m in range(MEMBERS):
        copy = pltpu.make_async_copy(anomalies.at[m, :, at], rest.at[m], sems.at[len(CHUNKS) * MEMBERS + m])
        copy.start()
        rest_copies.append(copy)
    time_copy.wait()
    at_zero = when[...].astype(F32).astype(BF16) == 0
    ws = [w[m] for m in range(MEMBERS)]
    for n, (first, count) in enumerate(CHUNKS):
        for copy in copies[n * MEMBERS : (n + 1) * MEMBERS]:
            copy.wait()

        def plane(r, c, first=first):
            total = None
            for m in range(MEMBERS):
                picked = jnp.where(at_zero, buf[m, 0, first + r], buf[m, 1, first + r])
                kept[m, first + r] = picked
                term = picked.astype(F32) * ws[m]
                total = term if total is None else total + term
            own[first + r] = total
            return c

        lax.fori_loop(0, count, plane, 0, unroll=5)
    for m, copy in enumerate(rest_copies):
        copy.wait()

        def plane_of_rest(r, c, m=m):
            later[m, r] = jnp.where(at_zero, rest[m, 0, r], rest[m, 1, r])
            return c

        lax.fori_loop(0, CHUNKS[1][1], plane_of_rest, 0, unroll=5)


def forward_body(chunk, ids, ext, rate_own, control, even, odd, loc_norm, sent1, sent2, w, rate, terms, *rest):
    sends, side, room = rest[:-2], rest[-2], rest[-1]
    halo = halo_of(MEMBERS + 1, ids, even, odd)
    lane = lax.broadcasted_iota(jnp.int32, (TALL, COLS), 1)
    near = (lane < REACH) | (lane >= COLS - REACH)
    rate_side = jnp.where(near, spread_halo(halo, MEMBERS), 0.0)
    rate[0] = rate_own[...]
    for sub in range(SUB):
        put(rate.at[1], sub, rate_side)
    for m in range(MEMBERS):
        put(side, m, spread_halo(halo, m))
    squares = jnp.zeros((ROWS, COLS), F32)
    for m in range(MEMBERS):
        squares = squares + control[m] * control[m]
    terms[...] = squares[:8] + squares[8:]
    for m, spread in enumerate(members_of(sweep(False, ext, side, rate), room)):
        w[m] = (loc_norm[...] * spread).astype(BF16).astype(F32)
    sends_body(chunk, ids, sent1, sent2, w, *sends)


def rides(chunk):
    return 1 if chunk == CHUNKS[-1] else 0


def misfit_body(chunk, factor, ids, own, got1, got2, got3, inn, prec, terms, weighted, *new_terms):
    first, count = chunk

    def plane(r, c):
        sums = (own[first + r] + got1[r].astype(F32)) + (got2[r].astype(F32) + got3[r].astype(F32))
        misfit = factor * sums - inn[first + r]
        scaled = prec[first + r] * misfit
        weighted[r] = scaled.astype(BF16)
        return c + misfit * scaled

    total = lax.fori_loop(0, count, plane, jnp.zeros((ROWS, COLS), F32), unroll=5 if count % 5 == 0 else 1)
    summed = terms[...] + (total[:8] + total[8:])
    if not rides(chunk):
        new_terms[0][...] = summed
    else:
        weighted[count] = split(summed)


def pull(sel, chunk, ref, acc):
    first, count = chunk

    def plane(r, acc):
        x = ref[r].astype(F32)
        return tuple(acc[m] + sel[m, first + r].astype(F32) * x for m in range(MEMBERS))

    return lax.fori_loop(0, count, plane, acc, unroll=5 if count % 5 == 0 else 1)


def own_pull_body(ids, kept, *rest):
    refs, new = rest[:-1], rest[-1]
    acc = tuple(jnp.zeros((ROWS, COLS), F32) for _ in range(MEMBERS))
    for chunk, ref in zip(CHUNKS, refs):
        acc = pull(kept, chunk, ref, acc)
    for m in range(MEMBERS):
        new[m] = acc[m]


def pull_all(chunk, sent1, later, old, refs):
    acc = tuple(old[m] for m in range(MEMBERS))
    parts = (sent1.at[0], chunk), (sent1.at[1], chunk), (later, (0, chunk[1]))
    for (sel, planes), ref in zip(parts, refs):
        acc = pull(sel, planes, ref, acc)
    return acc


RELAYED = 20


def pull_body(chunk, ids, sent1, sent2, old, ref1, ref2, ref3, ref4, new):
    first, count = chunk
    acc = tuple(old[m] for m in range(MEMBERS))
    acc = pull(sent1.at[0], (first, RELAYED), ref1, acc)
    acc = pull(sent1.at[0], (first + RELAYED, count - RELAYED), ref2, acc)
    acc = pull(sent1.at[1], chunk, ref3, acc)
    acc = pull(sent2.at[0], chunk, ref4, acc)
    for m in range(MEMBERS):
        new[m] = acc[m]


def last_pull_body(factor, ids, sent1, sent2, old, ref1, ref2, ref3, loc_norm, mine, new, halo, terms):
    acc = pull_all(CHUNKS[-1], sent1, sent2, old, (ref1, ref2, ref3))
    for m in range(MEMBERS):
        source = loc_norm[...] * (factor * acc[m])
        new[m] = source
        halo[m] = source.astype(BF16)
    at = CHUNKS[-1][1]
    summed = (ridden(mine[at]) + ridden(ref2[at])) + (ridden(ref3[at]) + ridden(ref1[at]))
    row = lax.broadcasted_iota(jnp.int32, (8, COLS), 0)
    plane = split(jnp.where(row == ids[1], jnp.sum(summed, axis=0, keepdims=True), 0.0))
    halo[MEMBERS] = plane
    terms[...] = ridden(plane)


def pass_body(ids, terms, even, odd, pair, passed):
    other = ridden(odd[TALL:])
    pair[:8] = terms[...] + ridden(even[TALL:])
    pair[8:] = other
    passed[...] = other


def finish_body(scale, ids, held, pair, got, far_pair, far_got, out, cost):
    mine = pair[:8] + (pair[8:] + got[...])
    far = far_pair[:8] + (far_pair[8:] + far_got[...])
    cost[...] = jnp.broadcast_to(jnp.sum(mine + far) * scale, (1, COLS))
    for m in range(MEMBERS):
        out[m] = held[m]


def adjoint_body(ids, ext, even, odd, rate, control, out, side, room):
    halo = halo_of(MEMBERS, ids, even, odd)
    for m in range(MEMBERS):
        put(side, m, spread_halo(halo, m))
    for m, back in enumerate(members_of(sweep(True, ext, side, rate), room)):
        out[m] = control[m] + back


def on_device(control, anomalies, diffusivity, loc_norm, innovation, obs_precision, obs_time):
    members = MEMBERS * lax.axis_size("mem")
    cells = members * ROWS * COLS * lax.axis_size("lat") * lax.axis_size("lon")
    factor = 1.0 / math.sqrt(members - 1)
    obs_time = in_hbm(obs_time)
    anomalies = in_hbm(anomalies.reshape(MEMBERS, 2, PLANES, ROWS, COLS))
    innovation = in_hbm(innovation.reshape(PLANES, ROWS, COLS))
    obs_precision = in_hbm(obs_precision.reshape(PLANES, ROWS, COLS))
    block = (MEMBERS, ROWS, COLS)

    (fields,) = call(
        join_body,
        [pltpu.VMEM((MEMBERS + 1, ROWS, COLS), BF16)],
        (in_hbm(control), in_hbm(diffusivity)),
        [ANY_SPEC] * 2,
        scratch=[pltpu.VMEM((MEMBERS + 1, ROWS, COLS), F32), pltpu.SemaphoreType.DMA((2,))],
        us=0.5,
    )
    even, odd = swap(fields, "lat", False), swap(fields, "lat", True)
    sent1, inn, prec = select(PARTNERS[:2], SHARE, anomalies, obs_time, (innovation, obs_precision))
    even, odd, sent1 = lax.optimization_barrier((even, odd, sent1))
    ext, rate, packed = pack(MEMBERS + 1, (control, diffusivity), even, odd)
    even, odd = swap(packed, "lon", False), swap(packed, "lon", True)
    (sent2,) = select(PARTNERS[2:], CHUNKS[0][1], anomalies, obs_time)
    even, odd, sent2 = lax.optimization_barrier((even, odd, sent2))

    def blocks(count):
        return [pltpu.VMEM((count, ROWS, COLS), BF16)] * 3

    tile = pltpu.VMEM((8, COLS), F32)
    w, rate, terms, *send = call(
        functools.partial(forward_body, CHUNKS[0]),
        [pltpu.VMEM(block, F32), pltpu.VMEM((2, *TILES), F32), tile, *blocks(CHUNKS[0][1])],
        (ext, rate, control, even, odd, loc_norm, sent1, sent2),
        [VMEM_SPEC] * 8,
        scratch=[pltpu.VMEM(TILES, F32), pltpu.VMEM((ROWS * SUB, COLS), F32)],
        us=2.0,
    )
    kept, own, later = call(
        stays_body,
        [
            pltpu.VMEM((MEMBERS, SHARE, ROWS, COLS), BF16),
            pltpu.VMEM((SHARE, ROWS, COLS), F32),
            pltpu.VMEM((MEMBERS, CHUNKS[1][1], ROWS, COLS), BF16),
        ],
        (anomalies, obs_time, w),
        [ANY_SPEC, ANY_SPEC, VMEM_SPEC],
        scratch=[
            pltpu.VMEM((MEMBERS, 2, SHARE, ROWS, COLS), BF16),
            pltpu.VMEM((MEMBERS, 2, CHUNKS[1][1], ROWS, COLS), BF16),
            pltpu.VMEM((ROWS, COLS), jnp.int32),
            pltpu.SemaphoreType.DMA(((len(CHUNKS) + 1) * MEMBERS,)),
            pltpu.SemaphoreType.DMA((1,)),
        ],
        limit=16 * MIB,
        us=2.0,
    )
    got = []
    for i, chunk in enumerate(CHUNKS):
        if i > 0:
            send = call(
                functools.partial(next_sends_body, chunk),
                blocks(chunk[1]),
                (sent1, later, w, own),
                [VMEM_SPEC] * 3 + [ANY_SPEC],
                us=0.3,
            )
        got.append([share(cells, p) for cells, p in zip(send, PARTNERS)])
    weighted, near = [], []
    for i, chunk in enumerate(CHUNKS):
        piece, *rest = call(
            functools.partial(misfit_body, chunk, factor),
            [pltpu.VMEM((chunk[1] + rides(chunk), ROWS, COLS), BF16)] + [tile] * (1 - rides(chunk)),
            (own, *got[i], inn, prec, terms),
            [VMEM_SPEC] * 7,
            us=0.3,
        )
        terms = rest[0] if rest else None
        weighted.append(piece)
        if i == len(CHUNKS) - 1:
            near.append([share(piece, p) for p in PARTNERS])
        else:
            a, b = share(piece, 1), share(piece, 3)
            near.append([share(b[:RELAYED], 1), share(a[RELAYED:], 3), a, b])
    (acc,) = call(
        own_pull_body,
        [pltpu.VMEM(block, F32)],
        (kept, *weighted),
        [VMEM_SPEC] * (1 + len(CHUNKS)),
        us=0.4,
    )
    for i, chunk in enumerate(CHUNKS[:-1]):
        (acc,) = call(
            functools.partial(pull_body, chunk),
            [pltpu.VMEM(block, F32)],
            (sent1, sent2, acc, *near[i]),
            [VMEM_SPEC] * 7,
            us=0.5,
        )
    source, halo, terms = call(
        functools.partial(last_pull_body, factor),
        [
            pltpu.VMEM(block, F32),
            pltpu.VMEM((MEMBERS + 1, ROWS, COLS), BF16),
            tile,
        ],
        (sent1, later, acc, *near[-1], loc_norm, weighted[-1]),
        [VMEM_SPEC] * 8,
        us=0.5,
    )
    got = trade(terms, ("lat",), (2, 3, 0, 1, 6, 7, 4, 5))
    even, odd = swap(halo, "lat", False), swap(halo, "lat", True)
    ext, packed, terms = pack(MEMBERS, (source, terms), even, odd)
    packed, terms = call(
        ride_body,
        [pltpu.VMEM((TALL + 16, COLS), BF16), tile],
        (packed, terms, got),
        [VMEM_SPEC] * 3,
        us=0.1,
        aliases={0: 0},
    )
    even, odd = swap(packed, "lon", False), swap(packed, "lon", True)
    pair, passed = call(
        pass_body, [pltpu.VMEM((16, COLS), F32), tile], (terms, even, odd), [VMEM_SPEC] * 3, us=0.1
    )
    got = swap(passed, "lon", False)
    far_pair = trade(pair, ("lat",), (4, 5, 6, 7, 0, 1, 2, 3))
    far_got = trade(passed, ("lat", "lon"), [(lat ^ 4) * 4 + (lon ^ 1) for lat in range(8) for lon in range(4)])
    even, odd, pair = lax.optimization_barrier((even, odd, pair))
    (held,) = call(
        adjoint_body,
        [pltpu.VMEM(block, F32)],
        (ext, even, odd, rate, control),
        [VMEM_SPEC] * 5,
        scratch=[pltpu.VMEM(TILES, F32), pltpu.VMEM((ROWS * SUB, COLS), F32)],
        us=3.0,
    )
    gradient, cost = call(
        functools.partial(finish_body, 0.5 / cells),
        [jax.ShapeDtypeStruct(block, F32), jax.ShapeDtypeStruct((1, COLS), F32)],
        (held, pair, got, far_pair, far_got),
        [VMEM_SPEC] * 5,
        us=0.1,
    )
    return gradient, cost[0, 0]


def solution(mesh):
    return jax.shard_map(
        on_device,
        mesh=mesh,
        in_specs=(
            P("mem", "lat", "lon"),
            P("mem", None, None, None, "lat", "lon"),
            P("lat", "lon"),
            P("lat", "lon"),
            P(None, None, "lat", "lon"),
            P(None, None, "lat", "lon"),
            P("lat", "lon"),
        ),
        out_specs=(P("mem", "lat", "lon"), P()),
        check_vma=False,
    )
```
